32 devices in a mesh: pipe: 4 (over y, core), tensor: 8 (over z, x).
Axes of the slice: x: 2, y: 2, z: 4, core: 2. Of those that a mesh axis runs over, the one named last changes fastest.
Arguments:
- inputs: bfloat16 [128, 4096], P(None, 'tensor'), may hold values from -6 to 6
- out_grad: bfloat16 [128, 4096], P(None, 'tensor'), may hold values from -6 to 6
- norm_gain: float32 [4, 4096], P('pipe'), may hold values from 0.25 to 1.75
- gate_weight: bfloat16 [4, 4096, 14336], P('pipe', None, 'tensor'), may hold values from -0.125 to 0.125
- up_weight: bfloat16 [4, 4096, 14336], P('pipe', None, 'tensor'), may hold values from -0.125 to 0.125
- down_weight: bfloat16 [4, 14336, 4096], P('pipe', 'tensor'), may hold values from -0.0625 to 0.0625
- block_mask: int32 [4, 3, 32, 112], P('pipe', None, None, 'tensor'), may hold values from 0 to 1, as said below
Outputs:
- section_out: float32 [4, 128, 4096], P('pipe')
- section_grad: float32 [4, 128, 4096], P('pipe')
The draws below stay inside these ranges and needn't reach their ends.
Inputs may be any that keep to these rules, and one draw needn't show every extreme that they name: `block_mask`: 1 keeps a block, 0 drops it; the share kept differs from one block column to another.
All inputs are finite; a program needn't handle non-finite values.
Results may differ from the reference program's by a relative error of at most 0.02.
Values may be sent and summed in bfloat16 or wider, within the bound.
No kernel may reach another device: no remote copies, remote signals or barrier semaphores. Data moves between devices by JAX's collectives and lax.ppermute only.
A program may use at most 192 MiB of HBM per device.

```python
import jax
import jax.numpy as jnp
from jax import lax

D = 4096
FF = 14336
BLOCK = 128
ROWS = 64
MB = 2
LAYERS = 4


def draw_block_mask(key, part):
    first, second = jax.random.split(jax.random.fold_in(key, 7))
    shape = (LAYERS, 3, D // BLOCK, FF // BLOCK)
    levels = jax.random.randint(first, (LAYERS, 3, 1, FF // BLOCK), 20, 81)
    draws = jax.random.randint(second, shape, 0, 100)
    return (draws < levels).astype(jnp.int32)


def shard_levels(own_key, shape, shards, low, high):
    level, own = 1.0, jax.random.fold_in(own_key, 6)
    for dim, shards_of in shards:
        steps = jnp.exp(jax.random.uniform(jax.random.fold_in(own, dim), (shards_of,), jnp.float32, low / len(shards), high / len(shards)))
        level = level * jnp.repeat(steps, shape[dim] // shards_of).reshape([-1 if axis == dim else 1 for axis in range(len(shape))])
    return level


def noise(own_key, shape, deviation, reach, pieces=(), kind=jnp.bfloat16):
    level = shard_levels(own_key, shape, pieces, -0.22, 0.18) if pieces else 1.0
    array = jax.random.normal(own_key, shape, jnp.float32) * deviation * level
    return jnp.minimum(jnp.maximum(array, -reach), reach).astype(kind)


def setup_inputs(seed: int = 0) -> dict:
    seeds = jax.random.split(jax.random.key(seed), 8)
    inputs = noise(seeds[0], (MB * ROWS, D), 1.0, 6.0, ((1, 8),))
    out_grad = noise(seeds[1], (MB * ROWS, D), 1.0, 6.0, ((1, 8),))
    norm_gain = jnp.clip(1.0 + 0.15 * jax.random.normal(seeds[2], (LAYERS, D), jnp.float32), 0.25, 1.75)
    gate_weight = noise(seeds[3], (LAYERS, D, FF), (D // 2) ** -0.5, 0.125, ((0, 4), (2, 8)))
    up_weight = noise(seeds[4], (LAYERS, D, FF), (D // 2) ** -0.5, 0.125, ((0, 4), (2, 8)))
    down_weight = noise(seeds[5], (LAYERS, FF, D), (FF // 2) ** -0.5, 0.0625, ((0, 4), (1, 8)))
    block_mask = draw_block_mask(jax.random.fold_in(seeds[7], 71), 0)
    return {"inputs": inputs, "out_grad": out_grad, "norm_gain": norm_gain, "gate_weight": gate_weight, "up_weight": up_weight, "down_weight": down_weight, "block_mask": block_mask}


def masked_blocks(weight, mask):
    rows, cols = weight.shape
    shaped = weight.reshape(rows // BLOCK, BLOCK, cols // BLOCK, BLOCK)
    return (shaped * mask.astype(weight.dtype)[:, None, :, None]).reshape(rows, cols)

def reference(inputs, out_grad, norm_gain, gate_weight, up_weight, down_weight, block_mask):
    eps = 1e-05
    state = inputs.astype(jnp.float32)
    saved = []
    outs_list = []
    for layer in range(LAYERS):
        gmat = masked_blocks(gate_weight[layer], block_mask[layer, 0])
        umat = masked_blocks(up_weight[layer], block_mask[layer, 1])
        dmat = masked_blocks(down_weight[layer], block_mask[layer, 2].T)
        xval = state
        scale = lax.rsqrt(lax.optimization_barrier(jnp.mean(xval * xval, axis=-1, keepdims=True)) + eps)
        normed = (xval * scale * norm_gain[layer]).astype(jnp.bfloat16)
        gate_matrix = jnp.dot(normed, gmat, preferred_element_type=jnp.float32)
        upval = jnp.dot(normed, umat, preferred_element_type=jnp.float32)
        hidden = (jax.nn.silu(gate_matrix) * upval).astype(jnp.bfloat16)
        branch = jnp.dot(hidden, dmat, preferred_element_type=jnp.float32)
        state = xval + branch
        outs_list.append(state)
        saved.append((xval, scale, gate_matrix, upval))
    grads_list = [None] * LAYERS
    cot = out_grad.astype(jnp.float32)
    for layer in range(LAYERS - 1, -1, -1):
        gmat = masked_blocks(gate_weight[layer], block_mask[layer, 0])
        umat = masked_blocks(up_weight[layer], block_mask[layer, 1])
        dmat = masked_blocks(down_weight[layer], block_mask[layer, 2].T)
        xval, scale, gate_matrix, upval = saved[layer]
        cot_low = cot.astype(jnp.bfloat16)
        dhid = jnp.dot(cot_low, dmat.T, preferred_element_type=jnp.float32)
        sig = jax.nn.sigmoid(gate_matrix)
        dgate = (dhid * upval * sig * (1.0 + gate_matrix * (1.0 - sig))).astype(jnp.bfloat16)
        dup = (dhid * gate_matrix * sig).astype(jnp.bfloat16)
        dnorm = jnp.dot(dgate, gmat.T, preferred_element_type=jnp.float32) + jnp.dot(dup, umat.T, preferred_element_type=jnp.float32)
        avec = dnorm * norm_gain[layer]
        inner = lax.optimization_barrier(jnp.mean(avec * xval, axis=-1, keepdims=True))
        back = scale * avec - xval * scale * scale * scale * inner
        cot = cot + back
        grads_list[layer] = cot
    return (jnp.stack(outs_list), jnp.stack(grads_list))
```

```python
import functools

import jax
import jax.numpy as jnp
from jax import lax
from jax.experimental import pallas as pl
from jax.experimental.pallas import tpu as pltpu
from jax.sharding import PartitionSpec as P

BLOCK = 128
EPS = 1e-05
F32 = jnp.float32
BF16 = jnp.bfloat16
VMEM_WHOLE = pl.BlockSpec(memory_space=pltpu.VMEM)
SMEM_WHOLE = pl.BlockSpec(memory_space=pltpu.SMEM)
HBM_WHOLE = pl.BlockSpec(memory_space=pltpu.HBM)


def tile_of(size):
    return next(tile for tile in (256, 128) if size % tile == 0)


def contract_last(left, right):
    return lax.dot_general(left, right, (((1,), (1,)), ((), ())), preferred_element_type=F32)


def load_kernel(mask, gate_hbm, up_hbm, down_hbm, gate_out, up_out, down_out, sems):
    width, cols = gate_out.shape
    parts = sems.shape[1]
    wide_rows, deep_rows = width // parts, cols // parts

    def bring(which, part):
        source, target = ((gate_hbm, gate_out), (up_hbm, up_out), (down_hbm, down_out))[which]
        size = deep_rows if which == 2 else wide_rows
        here = pl.ds(part * size, size)
        return pltpu.make_async_copy(source.at[0, here], target.at[here], sems.at[which, part])

    wide_blocks, deep_blocks = width // BLOCK, cols // BLOCK
    for which in range(3):
        for part in range(parts):
            bring(which, part).start()
    zero = jnp.zeros((BLOCK, BLOCK), BF16)
    for which, ref in ((0, gate_out), (1, up_out)):
        for part in range(parts):
            bring(which, part).wait()

            @pl.loop(part * (wide_blocks // parts), (part + 1) * (wide_blocks // parts))
            def _(row):
                for col in range(deep_blocks):

                    @pl.when(mask[(which * wide_blocks + row) * deep_blocks + col] == 0)
                    def _():
                        ref[pl.ds(row * BLOCK, BLOCK), col * BLOCK : (col + 1) * BLOCK] = zero

    for part in range(parts):
        bring(2, part).wait()

    @pl.loop(0, wide_blocks)
    def _(row):
        for col in range(deep_blocks):

            @pl.when(mask[(2 * wide_blocks + row) * deep_blocks + col] == 0)
            def _():
                down_out[col * BLOCK : (col + 1) * BLOCK, pl.ds(row * BLOCK, BLOCK)] = zero


def forward_kernel(flags, *refs, peers, stage):
    pieces = refs[:peers]
    gain, gmat, umat, dmat = refs[peers : peers + 4]
    xval, gate_store, up_store, partial, normed, hidden = refs[peers + 7 :]
    part = pieces[0].shape[1]
    width, cols = gmat.shape
    tile = tile_of(cols)

    @pl.when(flags[0] == stage)
    def _():
        for step in range(peers):
            place = lax.rem(flags[1] + peers - step, peers) * part
            xval[:, pl.ds(pl.multiple_of(place, part), part)] = pieces[step][...]

        def square(index, total):
            here = xval[:, pl.ds(pl.multiple_of(index * part, part), part)].astype(F32)
            return total + jnp.sum(here * here, axis=1, keepdims=True)

        total = lax.fori_loop(0, peers, square, jnp.zeros((xval.shape[0], 1), F32))
        scale = lax.rsqrt(total / width + EPS)

        @pl.loop(0, peers)
        def _(index):
            here = pl.ds(pl.multiple_of(index * part, part), part)
            normed[:, here] = (xval[:, here].astype(F32) * scale * gain[:, here]).astype(BF16)

        @pl.loop(0, cols // tile)
        def _(index):
            here = pl.ds(pl.multiple_of(index * tile, tile), tile)
            gate = jnp.dot(normed[...], gmat[:, here], preferred_element_type=F32)
            upper = jnp.dot(normed[...], umat[:, here], preferred_element_type=F32)
            gate_store[:, here] = gate
            up_store[:, here] = upper
            hidden[:, here] = (gate * jax.nn.sigmoid(gate) * upper).astype(BF16)

        @pl.loop(0, peers)
        def _(index):
            here = pl.ds(pl.multiple_of(index * part, part), part)
            partial[index] = jnp.dot(
                hidden[...], dmat[:, here], preferred_element_type=F32
            ).astype(BF16)


def backward_kernel(flags, *refs, peers, stage):
    pieces = refs[:peers]
    gain, gmat, umat, dmat, xval, gate_store, up_store = refs[peers : peers + 7]
    cot, partial, dgate, dup = refs[peers + 8 :]
    part = pieces[0].shape[1]
    width, cols = gmat.shape
    rows = xval.shape[0]
    tile = tile_of(cols)

    @pl.when(flags[0] == stage)
    def _():
        for step in range(peers):
            place = lax.rem(flags[1] + peers - step, peers) * part
            cot[:, pl.ds(pl.multiple_of(place, part), part)] = pieces[step][...]

        def square(index, total):
            here = xval[:, pl.ds(pl.multiple_of(index * part, part), part)].astype(F32)
            return total + jnp.sum(here * here, axis=1, keepdims=True)

        total = lax.fori_loop(0, peers, square, jnp.zeros((rows, 1), F32))
        scale = lax.rsqrt(total / width + EPS)

        def hidden_side(index, inner):
            here = pl.ds(pl.multiple_of(index * tile, tile), tile)
            dhid = contract_last(cot[...], dmat[here, :])
            gate = gate_store[:, here]
            upper = up_store[:, here]
            sig = jax.nn.sigmoid(gate)
            dgate_low = (dhid * upper * sig * (1.0 + gate * (1.0 - sig))).astype(BF16)
            dup_low = (dhid * gate * sig).astype(BF16)
            dgate[:, here] = dgate_low
            dup[:, here] = dup_low
            both = dgate_low.astype(F32) * gate + dup_low.astype(F32) * upper
            return inner + jnp.sum(both, axis=1, keepdims=True)

        inner = lax.fori_loop(0, cols // tile, hidden_side, jnp.zeros((rows, 1), F32))
        pull = scale * scale * inner / width

        @pl.loop(0, peers)
        def _(index):
            here = pl.ds(pl.multiple_of(index * part, part), part)
            dnorm = contract_last(dgate[...], gmat[here, :]) + contract_last(dup[...], umat[here, :])
            back = scale * (dnorm * gain[:, here]) - xval[:, here].astype(F32) * pull
            partial[index] = back.astype(BF16)


def local(inputs, out_grad, norm_gain, gate_weight, up_weight, down_weight, block_mask):
    stages, peers = lax.axis_size("pipe"), lax.axis_size("tensor")
    stage, peer = lax.axis_index("pipe"), lax.axis_index("tensor")
    rows, part = inputs.shape
    width, cols = gate_weight.shape[1:]
    flags = jnp.stack([stage, peer]).astype(jnp.int32)
    vmem = functools.partial(pltpu.CompilerParams, vmem_limit_bytes=14 * 2**20)

    gmat, umat, dmat = pl.pallas_call(
        load_kernel,
        out_shape=(
            pltpu.VMEM((width, cols), BF16),
            pltpu.VMEM((width, cols), BF16),
            pltpu.VMEM((cols, width), BF16),
        ),
        in_specs=[SMEM_WHOLE] + [HBM_WHOLE] * 3,
        out_specs=(VMEM_WHOLE,) * 3,
        scratch_shapes=[pltpu.SemaphoreType.DMA((3, 4))],
        compiler_params=vmem(),
        cost_estimate=pl.CostEstimate(flops=0, bytes_accessed=6 * width * cols, transcendentals=0),
        name="load_masked",
    )(block_mask.reshape(-1), gate_weight, up_weight, down_weight)

    in_vmem = functools.partial(pltpu.with_memory_space_constraint, memory_space=pltpu.VMEM)
    weights = [in_vmem(weight) for weight in (gmat, umat, dmat)]
    cost = pl.CostEstimate(
        flops=6 * rows * width * cols, bytes_accessed=6 * width * cols, transcendentals=0
    )
    partial_type = jax.ShapeDtypeStruct((peers, rows, part), BF16)
    hidden_type = pltpu.VMEM((rows, cols), F32)
    wide_type = pltpu.VMEM((rows, width), BF16)

    def forward(at, pieces, kept):
        return pl.pallas_call(
            functools.partial(forward_kernel, peers=peers, stage=at),
            out_shape=(wide_type, hidden_type, hidden_type, partial_type),
            in_specs=[SMEM_WHOLE] + [VMEM_WHOLE] * (peers + 7),
            out_specs=(VMEM_WHOLE,) * 4,
            scratch_shapes=[pltpu.VMEM((rows, width), BF16), pltpu.VMEM((rows, cols), BF16)],
            input_output_aliases={peers + 5: 0, peers + 6: 1, peers + 7: 2},
            compiler_params=vmem(),
            cost_estimate=cost,
            name="forward_layer",
        )(flags, *map(in_vmem, pieces), in_vmem(norm_gain), *weights, *map(in_vmem, kept))

    def backward(at, pieces, kept, cot):
        return pl.pallas_call(
            functools.partial(backward_kernel, peers=peers, stage=at),
            out_shape=(wide_type, partial_type),
            in_specs=[SMEM_WHOLE] + [VMEM_WHOLE] * (peers + 8),
            out_specs=(VMEM_WHOLE,) * 2,
            scratch_shapes=[pltpu.VMEM((rows, cols), BF16), pltpu.VMEM((rows, cols), BF16)],
            input_output_aliases={peers + 8: 0},
            compiler_params=vmem(),
            cost_estimate=cost,
            name="backward_layer",
        )(flags, *map(in_vmem, pieces), in_vmem(norm_gain), *weights, *map(in_vmem, kept), in_vmem(cot))

    def number(at, who):
        return at * peers + who

    def spread(value, routes, include_self):
        return [
            lax.ppermute(
                value,
                ("pipe", "tensor"),
                [
                    (number(source, who), number(target, (who + step) % peers))
                    for source, target in routes
                    for who in range(peers)
                ],
            )
            if step or include_self
            else value
            for step in range(peers)
        ]

    def summed(partial, whole):
        own = lax.dynamic_slice_in_dim(whole, peer * part, part, 1)
        arrived = lax.all_to_all(partial, "tensor", 0, 0)
        return (own.astype(F32) + jnp.sum(arrived.astype(F32), axis=0)).astype(BF16)

    first = jnp.where(stage == stages - 1, out_grad, inputs)
    ends = spread(first, [(0, 0), (stages - 1, stages - 1)], False)
    pieces = ends
    kept = (
        jnp.zeros((rows, width), BF16),
        jnp.zeros((rows, cols), F32),
        jnp.zeros((rows, cols), F32),
    )
    for at in range(stages):
        *kept, partial = forward(at, pieces, kept)
        if at < stages - 1:
            pieces = spread(summed(partial, kept[0]), [(at, at + 1)], True)
    last_partial = partial
    cot = jnp.zeros((rows, width), BF16)
    pieces = ends
    for at in range(stages - 1, -1, -1):
        cot, partial = backward(at, pieces, kept, cot)
        if at > 0:
            pieces = spread(summed(partial, cot), [(at, at - 1)], True)

    final = stage == stages - 1
    ends = spread(
        summed(jnp.where(final, last_partial, partial), jnp.where(final, kept[0], cot)),
        [(0, 0), (stages - 1, stages - 1)],
        False,
    )
    order = (peer - jnp.arange(peers)) % peers
    end = jnp.zeros((rows, peers, part), BF16).at[:, order].set(jnp.stack(ends, 1))
    end = end.reshape(rows, width)
    onward = lax.ppermute(kept[0], "pipe", [(at + 1, at) for at in range(stages - 1)])
    back = lax.ppermute(cot, "pipe", [(at, at + 1) for at in range(stages - 1)])
    section_out = jnp.where(final, end, onward).astype(F32)
    section_grad = jnp.where(stage == 0, end, back).astype(F32)
    return section_out[None], section_grad[None]


def solution(mesh):
    in_specs = (
        P(None, "tensor"),
        P(None, "tensor"),
        P("pipe", None),
        P("pipe", None, "tensor"),
        P("pipe", None, "tensor"),
        P("pipe", "tensor", None),
        P("pipe", None, None, "tensor"),
    )
    out_specs = (P("pipe", None, None), P("pipe", None, None))
    return jax.shard_map(local, mesh=mesh, in_specs=in_specs, out_specs=out_specs, check_vma=False)
```

```python
import functools

import jax
import jax.numpy as jnp
from jax import lax
from jax.experimental import pallas as pl
from jax.experimental.pallas import tpu as pltpu
from jax.sharding import PartitionSpec as P

BLOCK = 128
EPS = 1e-05
F32 = jnp.float32
BF16 = jnp.bfloat16
VMEM_WHOLE = pl.BlockSpec(memory_space=pltpu.VMEM)
SMEM_WHOLE = pl.BlockSpec(memory_space=pltpu.SMEM)
HBM_WHOLE = pl.BlockSpec(memory_space=pltpu.HBM)


def tile_of(size):
    return next(tile for tile in (256, 128) if size % tile == 0)


def load_kernel(mask, gate_hbm, up_hbm, down_hbm, *refs):
    gate_out, up_out, down_out, sems = refs[-4:]
    width, cols = gate_out.shape
    parts = sems.shape[1]
    wide_rows, deep_rows = width // parts, cols // parts

    def bring(which, part):
        source, target = ((gate_hbm, gate_out), (up_hbm, up_out), (down_hbm, down_out))[which]
        size = deep_rows if which == 2 else wide_rows
        here = pl.ds(part * size, size)
        return pltpu.make_async_copy(source.at[0, here], target.at[here], sems.at[which, part])

    wide_blocks, deep_blocks = width // BLOCK, cols // BLOCK
    for which in range(3):
        for part in range(parts):
            bring(which, part).start()
    zero = jnp.zeros((BLOCK, BLOCK), BF16)
    for which, ref in ((0, gate_out), (1, up_out)):
        for part in range(parts):
            bring(which, part).wait()

            @pl.loop(part * (wide_blocks // parts), (part + 1) * (wide_blocks // parts))
            def _(row):
                for col in range(deep_blocks):

                    @pl.when(mask[(which * wide_blocks + row) * deep_blocks + col] == 0)
                    def _():
                        ref[pl.ds(row * BLOCK, BLOCK), col * BLOCK : (col + 1) * BLOCK] = zero

    for part in range(parts):
        bring(2, part).wait()

    @pl.loop(0, wide_blocks)
    def _(row):
        for col in range(deep_blocks):

            @pl.when(mask[(2 * wide_blocks + row) * deep_blocks + col] == 0)
            def _():
                down_out[col * BLOCK : (col + 1) * BLOCK, pl.ds(row * BLOCK, BLOCK)] = zero


def place_pieces(flags, pieces, peers, part, store):
    for index in range(peers):
        if len(pieces) == 1:
            store(index * part, pieces[0][index])
        else:
            place = lax.rem(flags[1] + peers - index, peers) * part
            store(pl.multiple_of(place, part), pieces[index][...])


def forward_kernel(flags, *refs, peers, stage, count):
    pieces = refs[:count]
    gain, gmat, umat, dmat = refs[count : count + 4]
    xval, gate_store, up_store, partial, normed, hidden = refs[-6:]
    part = pieces[0].shape[-1]
    width, cols = gmat.shape
    tile = tile_of(cols)

    @pl.when(flags[0] == stage)
    def _():
        def store(place, value):
            xval[:, pl.ds(place, part)] = value

        place_pieces(flags, pieces, peers, part, store)

        def square(index, total):
            here = xval[:, pl.ds(pl.multiple_of(index * part, part), part)].astype(F32)
            return total + jnp.sum(here * here, axis=1, keepdims=True)

        total = lax.fori_loop(0, peers, square, jnp.zeros((xval.shape[0], 1), F32))
        scale = lax.rsqrt(total / width + EPS)

        @pl.loop(0, peers)
        def _(index):
            here = pl.ds(pl.multiple_of(index * part, part), part)
            normed[:, here] = (xval[:, here].astype(F32) * scale * gain[:, here]).astype(BF16)

        @pl.loop(0, cols // tile)
        def _(index):
            here = pl.ds(pl.multiple_of(index * tile, tile), tile)
            gate = jnp.dot(normed[...], gmat[:, here], preferred_element_type=F32)
            upper = jnp.dot(normed[...], umat[:, here], preferred_element_type=F32)
            gate_store[:, here] = gate
            up_store[:, here] = upper
            hidden[:, here] = (gate * jax.nn.sigmoid(gate) * upper).astype(BF16)

        @pl.loop(0, peers)
        def _(index):
            here = pl.ds(pl.multiple_of(index * part, part), part)
            partial[index] = jnp.dot(
                hidden[...], dmat[:, here], preferred_element_type=F32
            ).astype(BF16)


def sum_kernel(flags, arrived, whole, *refs, stage, axis):
    out = refs[-1]
    part = out.shape[axis]

    @pl.when(flags[0] == stage)
    def _():
        here = pl.ds(pl.multiple_of(flags[1] * part, part), part)
        total = (whole[:, here] if axis else whole[here, :]).astype(F32)
        for index in range(arrived.shape[0]):
            total = total + arrived[index].astype(F32)
        out[...] = total.astype(BF16)


def last_sum_kernel(flags, arrived, xval, cot, out, *, final):
    rows, part = out.shape
    here = pl.ds(pl.multiple_of(flags[1] * part, part), part)
    total = jnp.sum(arrived[...].astype(F32), axis=0)

    @pl.when(flags[0] == final)
    def _():
        out[...] = (total + xval[:, here].astype(F32)).astype(BF16)

    @pl.when(flags[0] != final)
    def _():
        out[...] = (total + cot[here, :].astype(F32).T).astype(BF16)


def last_partial_kernel(flags, last, partial, out, *, final):
    @pl.when(flags[0] == final)
    def _():
        out[...] = last[...]

    @pl.when(flags[0] != final)
    def _():
        @pl.loop(0, out.shape[0])
        def _(index):
            out[index] = partial[index].astype(F32).T.astype(BF16)


def outputs_kernel(flags, end, even_x, odd_x, even_cot, odd_cot, section_out, section_grad, *, final):
    peers, rows, part = end.shape
    odd = lax.rem(flags[0], 2) == 1

    def fill(condition, target, value):
        @pl.when(condition)
        def _():
            @pl.loop(0, peers)
            def _(index):
                here = pl.ds(pl.multiple_of(index * part, part), part)
                target[0, :, here] = value(index, here)

    fill(flags[0] == final, section_out, lambda index, here: end[index].astype(F32))
    fill((flags[0] != final) & odd, section_out, lambda index, here: odd_x[:, here].astype(F32))
    fill(
        (flags[0] != final) & jnp.logical_not(odd),
        section_out,
        lambda index, here: even_x[:, here].astype(F32),
    )
    fill(flags[0] == 0, section_grad, lambda index, here: end[index].astype(F32))
    fill((flags[0] != 0) & odd, section_grad, lambda index, here: even_cot[here, :].astype(F32).T)
    fill(
        (flags[0] != 0) & jnp.logical_not(odd),
        section_grad,
        lambda index, here: odd_cot[here, :].astype(F32).T,
    )


def turn_kernel(xval, gate, upper, xturned, gate_turned, up_turned):
    @pl.loop(0, xval.shape[1] // BLOCK)
    def _(index):
        here = pl.ds(pl.multiple_of(index * BLOCK, BLOCK), BLOCK)
        xturned[here, :] = xval[:, here].astype(F32).T.astype(BF16)

    @pl.loop(0, gate.shape[1] // BLOCK)
    def _(index):
        here = pl.ds(pl.multiple_of(index * BLOCK, BLOCK), BLOCK)
        gate_turned[here, :] = gate[:, here].T
        up_turned[here, :] = upper[:, here].T


def backward_kernel(flags, *refs, peers, stage, count):
    pieces = refs[:count]
    gain, gmat, umat, dmat, xval, gate_store, up_store = refs[count : count + 7]
    cot, partial, dgate, dup = refs[-4:]
    width, cols = gmat.shape
    part, rows = width // peers, xval.shape[1]
    tile = tile_of(cols)

    @pl.when(flags[0] == stage)
    def _():
        def store(place, value):
            cot[pl.ds(place, part), :] = value

        if count == 1:
            pltpu.sync_copy(pieces[0], cot)
        else:
            place_pieces(flags, pieces, peers, part, store)

        def square(index, total):
            here = xval[pl.ds(pl.multiple_of(index * part, part), part), :].astype(F32)
            return total + jnp.sum(here * here, axis=0, keepdims=True)

        total = lax.fori_loop(0, peers, square, jnp.zeros((1, rows), F32))
        scale = lax.rsqrt(total / width + EPS)

        def hidden_side(index, inner):
            here = pl.ds(pl.multiple_of(index * tile, tile), tile)
            dhid = jnp.dot(dmat[here, :], cot[...], preferred_element_type=F32)
            gate = gate_store[here, :]
            upper = up_store[here, :]
            sig = jax.nn.sigmoid(gate)
            dgate_low = (dhid * upper * sig * (1.0 + gate * (1.0 - sig))).astype(BF16)
            dup_low = (dhid * gate * sig).astype(BF16)
            dgate[here, :] = dgate_low
            dup[here, :] = dup_low
            both = dgate_low.astype(F32) * gate + dup_low.astype(F32) * upper
            return inner + jnp.sum(both, axis=0, keepdims=True)

        inner = lax.fori_loop(0, cols // tile, hidden_side, jnp.zeros((1, rows), F32))
        pull = scale * scale * inner / width

        @pl.loop(0, peers)
        def _(index):
            here = pl.ds(pl.multiple_of(index * part, part), part)
            dnorm = jnp.dot(gmat[here, :], dgate[...], preferred_element_type=F32) + jnp.dot(
                umat[here, :], dup[...], preferred_element_type=F32
            )
            back = scale * dnorm * gain[here, :] - xval[here, :].astype(F32) * pull
            partial[index] = back.astype(BF16)


def local(inputs, out_grad, norm_gain, gate_weight, up_weight, down_weight, block_mask):
    stages, peers = lax.axis_size("pipe"), lax.axis_size("tensor")
    stage, peer = lax.axis_index("pipe"), lax.axis_index("tensor")
    rows, part = inputs.shape
    width, cols = gate_weight.shape[1:]
    flags = jnp.stack([stage, peer]).astype(jnp.int32)
    vmem = functools.partial(pltpu.CompilerParams, vmem_limit_bytes=12 * 2**20)
    in_hbm = functools.partial(pltpu.with_memory_space_constraint, memory_space=pltpu.HBM)
    in_vmem = functools.partial(pltpu.with_memory_space_constraint, memory_space=pltpu.VMEM)

    tall_gain = jnp.broadcast_to(norm_gain.reshape(width, 1), (width, rows))
    grad_copies = jnp.broadcast_to(out_grad.T, (peers, part, rows))
    weights = pl.pallas_call(
        load_kernel,
        out_shape=(
            pltpu.VMEM((width, cols), BF16),
            pltpu.VMEM((width, cols), BF16),
            pltpu.VMEM((cols, width), BF16),
        ),
        in_specs=[SMEM_WHOLE] + [HBM_WHOLE] * 3 + [pl.BlockSpec(memory_space=pl.ANY), HBM_WHOLE, SMEM_WHOLE],
        out_specs=(VMEM_WHOLE,) * 3,
        scratch_shapes=[pltpu.SemaphoreType.DMA((3, 4))],
        compiler_params=vmem(),
        cost_estimate=pl.CostEstimate(flops=0, bytes_accessed=6 * width * cols, transcendentals=0),
        name="load_masked",
    )(block_mask.reshape(-1), gate_weight, up_weight, down_weight, tall_gain, in_hbm(grad_copies), flags)
    weights = [in_vmem(weight) for weight in weights]

    cost = pl.CostEstimate(
        flops=6 * rows * width * cols, bytes_accessed=6 * width * cols, transcendentals=0
    )
    small_cost = pl.CostEstimate(flops=0, bytes_accessed=4 * rows * width, transcendentals=0)
    hidden_type = pltpu.VMEM((rows, cols), F32)
    turned_type = pltpu.VMEM((cols, rows), F32)
    wide_type = pltpu.VMEM((rows, width), BF16)
    tall_type = pltpu.VMEM((width, rows), BF16)

    def forward(at, pieces, kept):
        count, held = len(pieces), len(kept)
        return pl.pallas_call(
            functools.partial(forward_kernel, peers=peers, stage=at, count=count),
            out_shape=(wide_type, hidden_type, hidden_type, jax.ShapeDtypeStruct((peers, rows, part), BF16)),
            in_specs=[SMEM_WHOLE] + [VMEM_WHOLE] * (count + 4 + held),
            out_specs=(VMEM_WHOLE,) * 4,
            scratch_shapes=[pltpu.VMEM((rows, width), BF16), pltpu.VMEM((rows, cols), BF16)],
            input_output_aliases={count + 5 + index: index for index in range(held)},
            compiler_params=vmem(),
            cost_estimate=cost,
            name="forward_layer",
        )(flags, *map(in_vmem, pieces), in_vmem(norm_gain), *weights, *map(in_vmem, kept))

    def backward(at, pieces, kept, cot):
        count, held = len(pieces), len(cot)
        return pl.pallas_call(
            functools.partial(backward_kernel, peers=peers, stage=at, count=count),
            out_shape=(tall_type, jax.ShapeDtypeStruct((peers, part, rows), BF16)),
            in_specs=[SMEM_WHOLE]
            + [HBM_WHOLE if count == 1 else VMEM_WHOLE] * count
            + [VMEM_WHOLE] * (7 + held),
            out_specs=(VMEM_WHOLE,) * 2,
            scratch_shapes=[pltpu.VMEM((cols, rows), BF16), pltpu.VMEM((cols, rows), BF16)],
            input_output_aliases={count + 8 + index: index for index in range(held)},
            compiler_params=vmem(),
            cost_estimate=cost,
            name="backward_layer",
        )(
            flags,
            *map(in_hbm if count == 1 else in_vmem, pieces),
            tall_gain,
            *weights,
            *map(in_vmem, kept),
            *map(in_vmem, cot),
        )

    def summed(at, partial, whole, axis, passed=()):
        arrived = lax.all_to_all(partial, "tensor", 0, 0)
        any_spec = HBM_WHOLE
        return pl.pallas_call(
            functools.partial(sum_kernel, stage=at, axis=axis),
            out_shape=[pltpu.HBM(value.shape, value.dtype) for value in passed]
            + [pltpu.VMEM(arrived.shape[1:], BF16)],
            in_specs=[SMEM_WHOLE] + [VMEM_WHOLE] * 2 + [any_spec] * len(passed),
            out_specs=[any_spec] * len(passed) + [VMEM_WHOLE],
            input_output_aliases={3 + index: index for index in range(len(passed))},
            compiler_params=vmem(),
            cost_estimate=small_cost,
            name="sum_pieces",
        )(flags, in_vmem(arrived), in_vmem(whole), *map(in_hbm, passed))

    def turned(kept):
        return pl.pallas_call(
            turn_kernel,
            out_shape=(tall_type, turned_type, turned_type),
            in_specs=[VMEM_WHOLE] * 3,
            out_specs=(VMEM_WHOLE,) * 3,
            compiler_params=vmem(),
            cost_estimate=small_cost,
            name="turn_kept",
        )(*map(in_vmem, kept))

    def moved(value, source, target, step):
        stride = target - source
        pairs = []
        for start in range(source % 2, stages, 2):
            if 0 <= start + stride < stages:
                pairs += [
                    (start * peers + who, (start + stride) * peers + (who + step) % peers)
                    for who in range(peers)
                ]
        return lax.ppermute(value, ("pipe", "tensor"), pairs)

    def spread(value, source, target):
        return [moved(value, source, target, step) for step in range(peers)]

    def gathered(shard):
        return lax.all_to_all(jnp.broadcast_to(shard, (peers,) + shard.shape), "tensor", 0, 0)

    kept, pieces = [], [gathered(inputs)]
    for at in range(stages):
        *kept, partial = forward(at, pieces, kept)
        if at < stages - 1:
            *passed, shard = summed(at, partial, kept[0], 1, () if at else (grad_copies,))
            if at == 0:
                last_pieces = [lax.all_to_all(passed[0], "tensor", 0, 0).reshape(width, rows)]
            pieces = spread(shard, at, at + 1)
    last_partial, xval = partial, kept[0]

    kept, cot, pieces = turned(kept), [], last_pieces
    for at in range(stages - 1, -1, -1):
        *cot, partial = backward(at, pieces, kept, cot)
        if at > 0:
            pieces = spread(summed(at, partial, cot[0], 0)[0], at, at - 1)
    cot = cot[0]

    final = stages - 1
    both = pl.pallas_call(
        functools.partial(last_partial_kernel, final=final),
        out_shape=pltpu.VMEM((peers, rows, part), BF16),
        in_specs=[SMEM_WHOLE] + [VMEM_WHOLE] * 2,
        out_specs=VMEM_WHOLE,
        compiler_params=vmem(),
        cost_estimate=small_cost,
        name="last_partial",
    )(flags, last_partial, in_vmem(partial))
    shard = pl.pallas_call(
        functools.partial(last_sum_kernel, final=final),
        out_shape=pltpu.VMEM((rows, part), BF16),
        in_specs=[SMEM_WHOLE] + [VMEM_WHOLE] * 3,
        out_specs=VMEM_WHOLE,
        compiler_params=vmem(),
        cost_estimate=small_cost,
        name="last_sum",
    )(flags, in_vmem(lax.all_to_all(both, "tensor", 0, 0)), in_vmem(xval), in_vmem(cot))
    end = gathered(shard)
    neighbours = (
        moved(xval, 1, 0, 0),
        moved(xval, 2, 1, 0),
        moved(cot, 0, 1, 0),
        moved(cot, 1, 2, 0),
    )
    return pl.pallas_call(
        functools.partial(outputs_kernel, final=final),
        out_shape=(jax.ShapeDtypeStruct((1, rows, width), F32),) * 2,
        in_specs=[SMEM_WHOLE] + [VMEM_WHOLE] * 5,
        out_specs=(VMEM_WHOLE,) * 2,
        compiler_params=vmem(vmem_limit_bytes=24 * 2**20),
        cost_estimate=small_cost,
        name="write_outputs",
    )(flags, end, *neighbours)


def solution(mesh):
    in_specs = (
        P(None, "tensor"),
        P(None, "tensor"),
        P("pipe", None),
        P("pipe", None, "tensor"),
        P("pipe", None, "tensor"),
        P("pipe", "tensor", None),
        P("pipe", None, None, "tensor"),
    )
    out_specs = (P("pipe", None, None), P("pipe", None, None))
    return jax.shard_map(local, mesh=mesh, in_specs=in_specs, out_specs=out_specs, check_vma=False)
```

```python
import functools

import jax
import jax.numpy as jnp
from jax import lax
from jax.experimental import pallas as pl
from jax.experimental.pallas import tpu as pltpu
from jax.sharding import PartitionSpec as P

BLOCK = 128
EPS = 1e-05
F32 = jnp.float32
BF16 = jnp.bfloat16
VMEM_WHOLE = pl.BlockSpec(memory_space=pltpu.VMEM)
SMEM_WHOLE = pl.BlockSpec(memory_space=pltpu.SMEM)
HBM_WHOLE = pl.BlockSpec(memory_space=pltpu.HBM)
FOUR_STAGE_SETS = (
    ((0, 2), (2, 1)),
    ((1, 2), (3, 1)),
    ((0, 1), (3, 2)),
    ((1, 3), (2, 0)),
)


def tile_of(size):
    return next(tile for tile in (256, 128) if size % tile == 0)


def contract_last(left, right):
    return lax.dot_general(left, right, (((1,), (1,)), ((), ())), preferred_element_type=F32)


def load_kernel(mask, gate_hbm, up_hbm, down_hbm, gate_out, up_out, down_out, sems):
    width, cols = gate_out.shape
    parts = sems.shape[1]
    wide_rows, deep_rows = width // parts, cols // parts

    def bring(which, part):
        source, target = ((gate_hbm, gate_out), (up_hbm, up_out), (down_hbm, down_out))[which]
        size = deep_rows if which == 2 else wide_rows
        here = pl.ds(part * size, size)
        return pltpu.make_async_copy(source.at[0, here], target.at[here], sems.at[which, part])

    wide_blocks, deep_blocks = width // BLOCK, cols // BLOCK
    for which in range(3):
        for part in range(parts):
            bring(which, part).start()
    zero = jnp.zeros((BLOCK, BLOCK), BF16)
    for which, ref in ((0, gate_out), (1, up_out)):
        for part in range(parts):
            bring(which, part).wait()

            @pl.loop(part * (wide_blocks // parts), (part + 1) * (wide_blocks // parts))
            def _(row):
                for col in range(deep_blocks):

                    @pl.when(mask[(which * wide_blocks + row) * deep_blocks + col] == 0)
                    def _():
                        ref[pl.ds(row * BLOCK, BLOCK), col * BLOCK : (col + 1) * BLOCK] = zero

    for part in range(parts):
        bring(2, part).wait()

    @pl.loop(0, wide_blocks)
    def _(row):
        for col in range(deep_blocks):

            @pl.when(mask[(2 * wide_blocks + row) * deep_blocks + col] == 0)
            def _():
                down_out[col * BLOCK : (col + 1) * BLOCK, pl.ds(row * BLOCK, BLOCK)] = zero


def place_of(flags, peers, part, step):
    return pl.multiple_of(lax.rem(flags[1] + peers + step, peers) * part, part)


def gather_pieces(flags, pieces, target):
    part = pieces[0].shape[1]
    for step, piece in enumerate(pieces):
        target[:, pl.ds(place_of(flags, len(pieces), part, -step), part)] = piece[...]


def row_scale(xval, peers):
    rows, width = xval.shape
    part = width // peers

    def square(index, total):
        here = xval[:, pl.ds(pl.multiple_of(index * part, part), part)].astype(F32)
        return total + jnp.sum(here * here, axis=1, keepdims=True)

    total = lax.fori_loop(0, peers, square, jnp.zeros((rows, 1), F32))
    return lax.rsqrt(total / width + EPS)


def pass_along(flags, source, extra, targets):
    if extra:

        @pl.when(flags[0] == source)
        def _():
            for step, target in enumerate(targets):
                target[...] = extra[step % len(extra)][...]


def forward_kernel(flags, *refs, peers, stage, held, source, extras):
    pieces = refs[:peers]
    gain, gmat, umat, dmat = refs[peers : peers + 4]
    extra = refs[peers + 4 + held : peers + 4 + held + extras]
    xval, gate_store, up_store, *partial = refs[peers + 4 + held + extras : -2]
    normed, hidden = refs[-2:]
    part = pieces[0].shape[1]
    width, cols = gmat.shape
    tile = tile_of(cols)
    pass_along(flags, source, extra, partial)

    @pl.when(flags[0] == stage)
    def _():
        gather_pieces(flags, pieces, xval)
        scale = row_scale(xval, peers)

        @pl.loop(0, peers)
        def _(index):
            here = pl.ds(pl.multiple_of(index * part, part), part)
            normed[:, here] = (xval[:, here].astype(F32) * scale * gain[:, here]).astype(BF16)

        @pl.loop(0, cols // tile)
        def _(index):
            here = pl.ds(pl.multiple_of(index * tile, tile), tile)
            gate = jnp.dot(normed[...], gmat[:, here], preferred_element_type=F32)
            upper = jnp.dot(normed[...], umat[:, here], preferred_element_type=F32)
            gate_store[:, here] = gate
            up_store[:, here] = upper
            hidden[:, here] = (gate * jax.nn.sigmoid(gate) * upper).astype(BF16)

        for step in range(peers):
            here = pl.ds(place_of(flags, peers, part, step), part)
            branch = jnp.dot(hidden[...], dmat[:, here], preferred_element_type=F32)
            if step == 0:
                branch = branch + xval[:, here].astype(F32)
            partial[step][...] = branch.astype(BF16)


def backward_kernel(flags, *refs, peers, stage, held, source, extras):
    pieces = refs[:peers]
    gain, gmat, umat, dmat, xval, gate_store, up_store = refs[peers : peers + 7]
    extra = refs[peers + 7 + held : peers + 7 + held + extras]
    cot, *partial = refs[peers + 7 + held + extras : -2]
    dgate, dup = refs[-2:]
    part = pieces[0].shape[1]
    rows = xval.shape[0]
    width, cols = gmat.shape
    tile = tile_of(cols)
    pass_along(flags, source, extra, partial)

    @pl.when(flags[0] == stage)
    def _():
        gather_pieces(flags, pieces, cot)
        scale = row_scale(xval, peers)

        def hidden_side(index, inner):
            here = pl.ds(pl.multiple_of(index * tile, tile), tile)
            dhid = contract_last(cot[...], dmat[here, :])
            gate = gate_store[:, here]
            upper = up_store[:, here]
            sig = jax.nn.sigmoid(gate)
            dgate_low = (dhid * upper * sig * (1.0 + gate * (1.0 - sig))).astype(BF16)
            dup_low = (dhid * gate * sig).astype(BF16)
            dgate[:, here] = dgate_low
            dup[:, here] = dup_low
            both = dgate_low.astype(F32) * gate + dup_low.astype(F32) * upper
            return inner + jnp.sum(both, axis=1, keepdims=True)

        inner = lax.fori_loop(0, cols // tile, hidden_side, jnp.zeros((rows, 1), F32))
        pull = scale * scale * inner / width

        for step in range(peers):
            here = pl.ds(place_of(flags, peers, part, step), part)
            dnorm = contract_last(dgate[...], gmat[here, :]) + contract_last(dup[...], umat[here, :])
            back = scale * (dnorm * gain[:, here]) - xval[:, here].astype(F32) * pull
            if step == 0:
                back = back + cot[:, here].astype(F32)
            partial[step][...] = back.astype(BF16)


def sum_kernel(flags, *refs, peers, owners, source):
    pieces, extra, out = refs[:peers], refs[peers:-1], refs[-1]
    active = functools.reduce(jnp.logical_or, [flags[0] == owner for owner in owners])

    @pl.when(active)
    def _():
        total = pieces[0][...].astype(F32)
        for piece in pieces[1:]:
            total = total + piece[...].astype(F32)
        out[...] = total.astype(BF16)

    pass_along(flags, source, extra, [out])


def outputs_kernel(flags, *refs, peers, counts):
    *sources, section_out, section_grad, low, sems = refs
    rows, width = low.shape
    part = width // peers
    start = 0
    for index, count in enumerate(counts):
        held = sources[start : start + count]
        start += count
        target = (section_out, section_grad)[index % 2]

        @pl.when(flags[0] == index // 2)
        def _():
            copies = []
            for step, source in enumerate(held):
                place = low
                if count > 1:
                    place = low.at[:, pl.ds(place_of(flags, peers, part, -step), part)]
                copies.append(pltpu.make_async_copy(source, place, sems.at[step]))
            for copy in copies:
                copy.start()
            for copy in copies:
                copy.wait()

            @pl.loop(0, peers)
            def _(number):
                here = pl.ds(pl.multiple_of(number * part, part), part)
                target[0, :, here] = low[:, here].astype(F32)


def local(inputs, out_grad, norm_gain, gate_weight, up_weight, down_weight, block_mask):
    stages, peers = lax.axis_size("pipe"), lax.axis_size("tensor")
    stage, peer = lax.axis_index("pipe"), lax.axis_index("tensor")
    rows, part = inputs.shape
    width, cols = gate_weight.shape[1:]
    final = stages - 1
    flags = jnp.stack([stage, peer]).astype(jnp.int32)
    vmem = functools.partial(pltpu.CompilerParams, vmem_limit_bytes=12 * 2**20)
    in_vmem = functools.partial(pltpu.with_memory_space_constraint, memory_space=pltpu.VMEM)
    in_hbm = functools.partial(pltpu.with_memory_space_constraint, memory_space=pltpu.HBM)

    if stages == 4:
        sets = FOUR_STAGE_SETS
    else:
        sets = tuple(((a, b),) for a in range(stages) for b in range(stages) if a != b)
    hops = [hop for group in sets for hop in group]

    def set_of(hop):
        return next(group for group in sets if hop in group)

    def owner_of(source, target):
        return next(o for o in range(stages) if (source, o) in hops and (o, target) in hops)

    def moved(value, hop, step):
        pairs = [
            (source * peers + who, target * peers + (who + step) % peers)
            for source, target in set_of(hop)
            for who in range(peers)
        ]
        return lax.ppermute(value, ("pipe", "tensor"), pairs)

    def spread(values, hop):
        return [moved(values[step % len(values)], hop, step) for step in range(peers)]

    waiting = []

    def fellow(hop):
        for entry in waiting:
            if entry[0] != hop and entry[0] in set_of(hop):
                waiting[:] = [other for other in waiting if other is not entry]
                return entry[:3]
        return (None, None), [], lambda arrived: None

    def piece_type():
        return pltpu.VMEM((rows, part), BF16)

    weights = pl.pallas_call(
        load_kernel,
        out_shape=(
            pltpu.VMEM((width, cols), BF16),
            pltpu.VMEM((width, cols), BF16),
            pltpu.VMEM((cols, width), BF16),
        ),
        in_specs=[SMEM_WHOLE] + [HBM_WHOLE] * 3,
        out_specs=(VMEM_WHOLE,) * 3,
        scratch_shapes=[pltpu.SemaphoreType.DMA((3, 4))],
        compiler_params=vmem(),
        cost_estimate=pl.CostEstimate(flops=0, bytes_accessed=6 * width * cols, transcendentals=0),
        name="load_masked",
    )(block_mask.reshape(-1), gate_weight, up_weight, down_weight)
    weights = [in_vmem(weight) for weight in weights]

    cost = pl.CostEstimate(
        flops=6 * rows * width * cols, bytes_accessed=6 * width * cols, transcendentals=0
    )
    small_cost = pl.CostEstimate(flops=0, bytes_accessed=4 * rows * width, transcendentals=0)
    hidden_type = pltpu.VMEM((rows, cols), F32)
    wide_type = pltpu.VMEM((rows, width), BF16)

    def layer(kernel, at, pieces, known, held, state_types, source, extra, name):
        operands = [*pieces, norm_gain, *known, *held, *extra]
        first_held = 1 + peers + 1 + len(known)
        outs = pl.pallas_call(
            functools.partial(
                kernel, peers=peers, stage=at, held=len(held), source=source, extras=len(extra)
            ),
            out_shape=(*state_types, *(piece_type() for _ in range(peers))),
            in_specs=[SMEM_WHOLE] + [VMEM_WHOLE] * len(operands),
            out_specs=(VMEM_WHOLE,) * (len(state_types) + peers),
            scratch_shapes=[pltpu.VMEM((rows, width if kernel is forward_kernel else cols), BF16)]
            + [pltpu.VMEM((rows, cols), BF16)],
            input_output_aliases={first_held + index: index for index in range(len(held))},
            compiler_params=vmem(),
            cost_estimate=cost,
            name=name,
        )(flags, *map(in_vmem, operands))
        return outs[: len(state_types)], outs[len(state_types) :]

    def summed(pieces, owners, source=None, extra=()):
        return pl.pallas_call(
            functools.partial(sum_kernel, peers=peers, owners=owners, source=source),
            out_shape=piece_type(),
            in_specs=[SMEM_WHOLE] + [VMEM_WHOLE] * (peers + len(extra)),
            out_specs=VMEM_WHOLE,
            compiler_params=vmem(vmem_limit_bytes=2*2**20),
            cost_estimate=small_cost,
            name="sum_pieces",
        )(flags, *map(in_vmem, pieces), *map(in_vmem, extra))

    section_out, section_grad = [None] * stages, [None] * stages

    def keep_in(store, at):
        def arrive(arrived):
            store[at] = arrived

        return arrive

    def handed(at, target, run, store):
        owner = owner_of(at, target)
        (source, _), extra, arrive = fellow((at, owner))
        pieces = spread(run(source, extra), (at, owner))
        late = arrive(pieces)
        (source, _), extra, arrive = fellow((owner, target))
        if late is not None and (late, final) in set_of((owner, target)) and not extra:
            shard = summed(pieces, (owner, late))
            arrive = keep_in(section_out, final)
        else:
            shard = summed(pieces, (owner,), source, extra)
            if late is not None:
                waiting.append(
                    ((late, final), [summed(pieces, (late,))], keep_in(section_out, final), None)
                )
        if target != at:
            waiting.append(((owner, at), [shard], keep_in(store, at), store))
        got = spread([shard], (owner, target))
        arrive(got)
        return got

    first_from = next(a for a, b in hops if b == 0)
    last_from = next(a for a, b in hops if b == final)
    if set_of((first_from, 0)) == set_of((last_from, final)):
        first = jnp.where(stage == last_from, out_grad, inputs)
        pieces = last_pieces = spread([first], (first_from, 0))
    else:
        pieces, last_pieces = spread([inputs], (first_from, 0)), spread([out_grad], (last_from, final))

    kept = []

    def run_forward(at, pieces, source, extra):
        nonlocal kept
        kept, partial = layer(
            forward_kernel, at, pieces, weights, kept,
            (wide_type, hidden_type, hidden_type), source, extra, "forward_layer",
        )
        return partial

    for at in range(final):
        pieces = handed(at, at + 1, functools.partial(run_forward, at, pieces), section_out)
    last_partial = run_forward(final, pieces, None, [])
    last_owner = owner_of(final, final)
    waiting.append(((final, last_owner), last_partial, lambda arrived: last_owner, None))

    cot = []

    def run_backward(at, pieces, source, extra):
        nonlocal cot
        cot, partial = layer(
            backward_kernel, at, pieces, (*weights, *kept), cot, (wide_type,), source, extra, "backward_layer"
        )
        return partial

    pieces = last_pieces
    for at in range(final, -1, -1):
        pieces = handed(at, max(at - 1, 0), functools.partial(run_backward, at, pieces), section_grad)
        for entry in tuple(waiting):
            if at and entry[0][1] == at + 1 and entry[3] is section_grad and (at, at + 1) in hops:
                waiting[:] = [other for other in waiting if other is not entry]
                section_grad[at + 1] = [moved(cot[0], (at, at + 1), 0)]
    section_grad[0] = pieces

    while waiting:
        hop, values, arrive, _ = waiting.pop(0)
        arrived = spread(values, hop)
        late = arrive(arrived)
        if late is not None:
            waiting.append(((late, final), [summed(arrived, (late,))], keep_in(section_out, final), None))

    sources = [store[at] for at in range(stages) for store in (section_out, section_grad)]
    flat = [value for source in sources for value in source]
    return pl.pallas_call(
        functools.partial(outputs_kernel, peers=peers, counts=[len(source) for source in sources]),
        out_shape=(jax.ShapeDtypeStruct((1, rows, width), F32),) * 2,
        in_specs=[SMEM_WHOLE] + [HBM_WHOLE] * len(flat),
        out_specs=(VMEM_WHOLE,) * 2,
        scratch_shapes=[pltpu.VMEM((rows, width), BF16), pltpu.SemaphoreType.DMA((peers,))],
        compiler_params=vmem(),
        cost_estimate=small_cost,
        name="write_outputs",
    )(flags, *map(in_hbm, flat))


def solution(mesh):
    in_specs = (
        P(None, "tensor"),
        P(None, "tensor"),
        P("pipe", None),
        P("pipe", None, "tensor"),
        P("pipe", None, "tensor"),
        P("pipe", "tensor", None),
        P("pipe", None, None, "tensor"),
    )
    out_specs = (P("pipe", None, None), P("pipe", None, None))
    return jax.shard_map(local, mesh=mesh, in_specs=in_specs, out_specs=out_specs, check_vma=False)
```

```python
import functools

import jax
import jax.numpy as jnp
from jax import lax
from jax.experimental import pallas as pl
from jax.experimental.pallas import tpu as pltpu
from jax.sharding import PartitionSpec as P

BLOCK = 128
EPS = 1e-05
F32 = jnp.float32
BF16 = jnp.bfloat16
VMEM_WHOLE = pl.BlockSpec(memory_space=pltpu.VMEM)
SMEM_WHOLE = pl.BlockSpec(memory_space=pltpu.SMEM)
HBM_WHOLE = pl.BlockSpec(memory_space=pltpu.HBM)
FOUR_STAGE_SETS = (
    ((0, 2), (2, 1)),
    ((1, 2), (3, 1)),
    ((0, 1), (3, 2)),
    ((1, 3), (2, 0)),
)


def tile_of(size):
    return next(tile for tile in (256, 128) if size % tile == 0)


def contract_last(left, right):
    return lax.dot_general(left, right, (((1,), (1,)), ((), ())), preferred_element_type=F32)


def load_kernel(mask, gate_hbm, up_hbm, down_hbm, gate_out, up_out, down_out, sems):
    width, cols = gate_out.shape
    parts = sems.shape[1]
    wide_rows, deep_rows = width // parts, cols // parts

    def bring(which, part):
        source, target = ((gate_hbm, gate_out), (up_hbm, up_out), (down_hbm, down_out))[which]
        size = deep_rows if which == 2 else wide_rows
        here = pl.ds(part * size, size)
        return pltpu.make_async_copy(source.at[0, here], target.at[here], sems.at[which, part])

    wide_blocks, deep_blocks = width // BLOCK, cols // BLOCK
    for which in range(3):
        for part in range(parts):
            bring(which, part).start()
    zero = jnp.zeros((BLOCK, BLOCK), BF16)
    for which, ref in ((0, gate_out), (1, up_out)):
        for part in range(parts):
            bring(which, part).wait()

            @pl.loop(part * (wide_blocks // parts), (part + 1) * (wide_blocks // parts))
            def _(row):
                for col in range(deep_blocks):

                    @pl.when(mask[(which * wide_blocks + row) * deep_blocks + col] == 0)
                    def _():
                        ref[pl.ds(row * BLOCK, BLOCK), col * BLOCK : (col + 1) * BLOCK] = zero

    for part in range(parts):
        bring(2, part).wait()

    @pl.loop(0, wide_blocks)
    def _(row):
        for col in range(deep_blocks):

            @pl.when(mask[(2 * wide_blocks + row) * deep_blocks + col] == 0)
            def _():
                down_out[col * BLOCK : (col + 1) * BLOCK, pl.ds(row * BLOCK, BLOCK)] = zero


def place_of(flags, peers, part, step):
    return pl.multiple_of(lax.rem(flags[1] + peers + step, peers) * part, part)


def row_scale(xval, peers):
    rows, width = xval.shape
    part = width // peers

    def square(index, total):
        here = xval[:, pl.ds(pl.multiple_of(index * part, part), part)].astype(F32)
        return total + jnp.sum(here * here, axis=1, keepdims=True)

    total = lax.fori_loop(0, peers, square, jnp.zeros((rows, 1), F32))
    return lax.rsqrt(total / width + EPS)


def pass_along(flags, source, extra, targets):
    if extra:

        @pl.when(flags[0] == source)
        def _():
            for step, target in enumerate(targets):
                target[...] = extra[step % len(extra)][...]


def forward_in_kernel(flags, gmat, umat, dmat, *refs, peers, stage, held, steps, ends):
    count = len(steps)
    pieces = refs[:count]
    gain = refs[count]
    xval, gate_store, up_store, *hidden, scaled = refs[count + 1 + held :]
    part = pieces[0].shape[1]
    width, cols = gmat.shape
    tile = tile_of(cols)

    @pl.when(flags[0] == stage)
    def _():
        places = [place_of(flags, peers, part, -step) for step in steps]
        for index, piece in enumerate(pieces):
            here = pl.ds(places[index], part)
            xval[:, here] = piece[...]
            scaled[index] = (piece[...].astype(F32) * gain[:, here]).astype(BF16)
        scale = row_scale(xval, peers) if ends else None

        @pl.loop(0, cols // tile)
        def _(number):
            here = pl.ds(pl.multiple_of(number * tile, tile), tile)
            totals = []
            for store, mat in ((gate_store, gmat), (up_store, umat)):
                total = store[:, here] if ends else None
                for index in range(count):
                    term = jnp.dot(
                        scaled[index], mat[pl.ds(places[index], part), here], preferred_element_type=F32
                    )
                    total = term if total is None else total + term
                if ends:
                    total = total * scale
                store[:, here] = total
                totals.append(total)
            if ends:
                gate, upper = totals
                hidden[0][:, here] = (gate * jax.nn.sigmoid(gate) * upper).astype(BF16)


def forward_out_kernel(flags, gmat, umat, dmat, *refs, peers, stage, steps, source, extras):
    hidden, xval = refs[:2]
    extra, partial = refs[2 : 2 + extras], refs[-len(steps) :]
    part = partial[0].shape[1]
    pass_along(flags, source, extra, partial)

    @pl.when(flags[0] == stage)
    def _():
        for step, target in zip(steps, partial):
            here = pl.ds(place_of(flags, peers, part, step), part)
            branch = jnp.dot(hidden[...], dmat[:, here], preferred_element_type=F32)
            if step == 0:
                branch = branch + xval[:, here].astype(F32)
            target[...] = branch.astype(BF16)


def backward_in_kernel(flags, gmat, umat, dmat, *refs, peers, stage, held, steps, ends):
    count = len(steps)
    pieces = refs[:count]
    xval, gate_store, up_store = refs[count : count + 3]
    cot, dhid_store, *outs = refs[count + 3 + held :]
    part = pieces[0].shape[1]
    rows, width = xval.shape
    cols = dmat.shape[0]
    tile = tile_of(cols)

    @pl.when(flags[0] == stage)
    def _():
        places = [place_of(flags, peers, part, -step) for step in steps]
        for index, piece in enumerate(pieces):
            cot[:, pl.ds(places[index], part)] = piece[...]

        def hidden_side(number, inner):
            here = pl.ds(pl.multiple_of(number * tile, tile), tile)
            dhid = dhid_store[:, here] if ends else None
            for index, piece in enumerate(pieces):
                term = contract_last(piece[...], dmat[here, pl.ds(places[index], part)])
                dhid = term if dhid is None else dhid + term
            if not ends:
                dhid_store[:, here] = dhid
                return inner
            gate = gate_store[:, here]
            upper = up_store[:, here]
            sig = jax.nn.sigmoid(gate)
            dgate_low = (dhid * upper * sig * (1.0 + gate * (1.0 - sig))).astype(BF16)
            dup_low = (dhid * gate * sig).astype(BF16)
            outs[0][:, here] = dgate_low
            outs[1][:, here] = dup_low
            both = dgate_low.astype(F32) * gate + dup_low.astype(F32) * upper
            return inner + jnp.sum(both, axis=1, keepdims=True)

        inner = lax.fori_loop(0, cols // tile, hidden_side, jnp.zeros((rows, 1), F32))
        if ends:
            scale = row_scale(xval, peers)
            lanes = outs[2].shape[1] // 2
            outs[2][:, :lanes] = jnp.broadcast_to(scale, (rows, lanes))
            outs[2][:, lanes:] = jnp.broadcast_to(scale * scale * inner / width, (rows, lanes))


def backward_out_kernel(flags, gmat, umat, dmat, *refs, peers, stage, steps, source, extras):
    dgate, dup, scales, xval, cot, gain = refs[:6]
    extra, partial = refs[6 : 6 + extras], refs[-len(steps) :]
    part = partial[0].shape[1]
    pass_along(flags, source, extra, partial)

    @pl.when(flags[0] == stage)
    def _():
        lanes = scales.shape[1] // 2
        scale, pull = scales[:, :1], scales[:, lanes : lanes + 1]
        for step, target in zip(steps, partial):
            here = pl.ds(place_of(flags, peers, part, step), part)
            dnorm = contract_last(dgate[...], gmat[here, :]) + contract_last(dup[...], umat[here, :])
            back = scale * (dnorm * gain[:, here]) - xval[:, here].astype(F32) * pull
            if step == 0:
                back = back + cot[:, here].astype(F32)
            target[...] = back.astype(BF16)


def sum_kernel(flags, *refs, peers, owners, source):
    pieces, extra, out = refs[:peers], refs[peers:-1], refs[-1]
    active = functools.reduce(jnp.logical_or, [flags[0] == owner for owner in owners])

    @pl.when(active)
    def _():
        total = pieces[0][...].astype(F32)
        for piece in pieces[1:]:
            total = total + piece[...].astype(F32)
        out[...] = total.astype(BF16)

    pass_along(flags, source, extra, [out])


def outputs_kernel(flags, *refs, peers, counts):
    *sources, section_out, section_grad, low, sems = refs
    rows, width = low.shape
    part = width // peers
    start = 0
    for index, count in enumerate(counts):
        held = sources[start : start + count]
        start += count
        target = (section_out, section_grad)[index % 2]

        @pl.when(flags[0] == index // 2)
        def _():
            copies = []
            for step, source in enumerate(held):
                place = low
                if count > 1:
                    place = low.at[:, pl.ds(place_of(flags, peers, part, -step), part)]
                copies.append(pltpu.make_async_copy(source, place, sems.at[step]))
            for copy in copies:
                copy.start()
            for copy in copies:
                copy.wait()

            @pl.loop(0, peers)
            def _(number):
                here = pl.ds(pl.multiple_of(number * part, part), part)
                target[0, :, here] = low[:, here].astype(F32)


def local(inputs, out_grad, norm_gain, gate_weight, up_weight, down_weight, block_mask):
    stages, peers = lax.axis_size("pipe"), lax.axis_size("tensor")
    stage, peer = lax.axis_index("pipe"), lax.axis_index("tensor")
    rows, part = inputs.shape
    width, cols = gate_weight.shape[1:]
    final = stages - 1
    flags = jnp.stack([stage, peer]).astype(jnp.int32)
    vmem = functools.partial(pltpu.CompilerParams, vmem_limit_bytes=12 * 2**20)
    in_vmem = functools.partial(pltpu.with_memory_space_constraint, memory_space=pltpu.VMEM)
    in_hbm = functools.partial(pltpu.with_memory_space_constraint, memory_space=pltpu.HBM)

    if stages == 4:
        sets = FOUR_STAGE_SETS
    else:
        sets = tuple(((a, b),) for a in range(stages) for b in range(stages) if a != b)
    hops = [hop for group in sets for hop in group]

    def set_of(hop):
        return next(group for group in sets if hop in group)

    def owner_of(source, target):
        return next(o for o in range(stages) if (source, o) in hops and (o, target) in hops)

    def moved(value, hop, step):
        pairs = [
            (source * peers + who, target * peers + (who + step) % peers)
            for source, target in set_of(hop)
            for who in range(peers)
        ]
        return lax.ppermute(value, ("pipe", "tensor"), pairs)

    def spread(values, hop):
        return [moved(values[step % len(values)], hop, step) for step in range(peers)]

    waiting = []

    def fellow(hop):
        for entry in waiting:
            if entry[0] != hop and entry[0] in set_of(hop):
                waiting[:] = [other for other in waiting if other is not entry]
                return entry[:3]
        return (None, None), [], lambda arrived: None

    def piece_type():
        return pltpu.VMEM((rows, part), BF16)

    weights = pl.pallas_call(
        load_kernel,
        out_shape=(
            pltpu.VMEM((width, cols), BF16),
            pltpu.VMEM((width, cols), BF16),
            pltpu.VMEM((cols, width), BF16),
        ),
        in_specs=[SMEM_WHOLE] + [HBM_WHOLE] * 3,
        out_specs=(VMEM_WHOLE,) * 3,
        scratch_shapes=[pltpu.SemaphoreType.DMA((3, 4))],
        compiler_params=vmem(vmem_limit_bytes=13 * 2**20),
        cost_estimate=pl.CostEstimate(flops=0, bytes_accessed=6 * width * cols, transcendentals=0),
        name="load_masked",
    )(block_mask.reshape(-1), gate_weight, up_weight, down_weight)
    weights = [in_vmem(weight) for weight in weights]

    small_cost = pl.CostEstimate(flops=0, bytes_accessed=4 * rows * width, transcendentals=0)
    hidden_type = pltpu.VMEM((rows, cols), F32)
    wide_type = pltpu.VMEM((rows, width), BF16)

    order = sorted(range(peers), key=lambda step: (abs(2 * step - peers), step))
    halves = (tuple(order[: peers // 2]), tuple(order[peers // 2 :]))

    def called(kernel, operands, carried, out_types, scratch, name, share, **known):
        held_from = 1 + len(weights) + len(operands)
        return pl.pallas_call(
            functools.partial(kernel, peers=peers, **known),
            out_shape=tuple(out_types),
            in_specs=[SMEM_WHOLE] * 1 + [VMEM_WHOLE] * (len(weights) + len(operands) + len(carried)),
            out_specs=(VMEM_WHOLE,) * len(out_types),
            scratch_shapes=scratch,
            input_output_aliases={held_from + index: index for index in range(len(carried))},
            compiler_params=vmem(vmem_limit_bytes=13 * 2**20),
            cost_estimate=pl.CostEstimate(
                flops=int(share * 2 * rows * width * cols),
                bytes_accessed=int(share * 2 * width * cols),
                transcendentals=0,
            ),
            name=name,
        )(flags, *weights, *map(in_vmem, operands), *map(in_vmem, carried))

    def pieces_out(kernel, at, operands, source, extra, groups, share, name):
        partial = [None] * peers
        for steps in groups:
            own = [extra[step % len(extra)] for step in steps] if len(extra) > 1 else list(extra)
            outs = called(
                kernel, [*operands, *own], [], [piece_type() for _ in steps], [], name,
                share * len(steps) / peers, stage=at, steps=steps, source=source, extras=len(own),
            )
            for step, out in zip(steps, outs):
                partial[step] = out
        return partial

    def summed(pieces, owners, source=None, extra=()):
        return pl.pallas_call(
            functools.partial(sum_kernel, peers=peers, owners=owners, source=source),
            out_shape=piece_type(),
            in_specs=[SMEM_WHOLE] + [VMEM_WHOLE] * (peers + len(extra)),
            out_specs=VMEM_WHOLE,
            compiler_params=vmem(vmem_limit_bytes=2*2**20),
            cost_estimate=small_cost,
            name="sum_pieces",
        )(flags, *map(in_vmem, pieces), *map(in_vmem, extra))

    section_out, section_grad = [None] * stages, [None] * stages

    def keep_in(store, at):
        def arrive(arrived):
            store[at] = arrived

        return arrive

    def handed(at, target, run, store):
        owner = owner_of(at, target)
        (source, _), extra, arrive = fellow((at, owner))
        pieces = spread(run(source, extra), (at, owner))
        late = arrive(pieces)
        (source, _), extra, arrive = fellow((owner, target))
        if late is not None and (late, final) in set_of((owner, target)) and not extra:
            shard = summed(pieces, (owner, late))
            arrive = keep_in(section_out, final)
        else:
            shard = summed(pieces, (owner,), source, extra)
            if late is not None:
                waiting.append(
                    ((late, final), [summed(pieces, (late,))], keep_in(section_out, final), None)
                )
        if target != at:
            waiting.append(((owner, at), [shard], keep_in(store, at), store))
        got = spread([shard], (owner, target))
        arrive(got)
        return got

    first_from = next(a for a, b in hops if b == 0)
    last_from = next(a for a, b in hops if b == final)
    if set_of((first_from, 0)) == set_of((last_from, final)):
        first = jnp.where(stage == last_from, out_grad, inputs)
        pieces = last_pieces = spread([first], (first_from, 0))
    else:
        pieces, last_pieces = spread([inputs], (first_from, 0)), spread([out_grad], (last_from, final))

    kept = []
    gmat, umat, dmat = weights

    def forward_in(at, pieces):
        nonlocal kept
        for steps in halves:
            ends = steps is halves[-1]
            types = [wide_type, hidden_type, hidden_type] + [pltpu.VMEM((rows, cols), BF16)] * ends
            outs = called(
                forward_in_kernel, [*(pieces[step] for step in steps), norm_gain], kept, types,
                [pltpu.VMEM((len(steps), rows, part), BF16)], "forward_in", 1.0,
                stage=at, held=len(kept), steps=steps, ends=ends,
            )
            kept = outs[:3]
        return outs[3]

    def forward_out(at, hidden, xval, source, extra):
        return pieces_out(
            forward_out_kernel, at, [hidden, xval], source, extra, halves, 1.0, "forward_out"
        )

    def run_forward(at, pieces, source, extra):
        return forward_out(at, forward_in(at, pieces), kept[0], source, extra)

    for at in range(final):
        pieces = handed(at, at + 1, functools.partial(run_forward, at, pieces), section_out)
    last_hidden = forward_in(final, pieces)

    cot = []
    quarters = tuple(half[at : at + max(1, peers // 4)] for half in halves for at in range(0, len(half), max(1, peers // 4)))

    def run_backward(at, pieces, source, extra):
        nonlocal cot
        low_type = pltpu.VMEM((rows, cols), BF16)
        for steps in halves:
            ends = steps is halves[-1]
            types = [wide_type, hidden_type] + [low_type, low_type, pltpu.VMEM((rows, 2 * BLOCK), F32)] * ends
            outs = called(
                backward_in_kernel, [*(pieces[step] for step in steps), *kept], cot, types, [],
                "backward_in", 0.5, stage=at, held=len(cot), steps=steps, ends=ends,
            )
            cot = outs[:2]
        partial = pieces_out(
            backward_out_kernel, at, [*outs[2:], kept[0], cot[0], norm_gain],
            source, extra, quarters, 2.0, "backward_out",
        )
        if at == final:
            last_owner = owner_of(final, final)
            hidden, xval, *_ = lax.optimization_barrier((last_hidden, kept[0], partial[order[-1]]))
            last_partial = forward_out(final, hidden, xval, None, [])
            waiting.append(((final, last_owner), last_partial, lambda arrived: last_owner, None))
        return partial

    pieces = last_pieces
    for at in range(final, -1, -1):
        pieces = handed(at, max(at - 1, 0), functools.partial(run_backward, at, pieces), section_grad)
        for entry in tuple(waiting):
            if at and entry[0][1] == at + 1 and entry[3] is section_grad and (at, at + 1) in hops:
                waiting[:] = [other for other in waiting if other is not entry]
                section_grad[at + 1] = [moved(cot[0], (at, at + 1), 0)]
    section_grad[0] = pieces

    while waiting:
        hop, values, arrive, _ = waiting.pop(0)
        arrived = spread(values, hop)
        late = arrive(arrived)
        if late is not None:
            waiting.append(((late, final), [summed(arrived, (late,))], keep_in(section_out, final), None))

    sources = [store[at] for at in range(stages) for store in (section_out, section_grad)]
    flat = [value for source in sources for value in source]
    return pl.pallas_call(
        functools.partial(outputs_kernel, peers=peers, counts=[len(source) for source in sources]),
        out_shape=(jax.ShapeDtypeStruct((1, rows, width), F32),) * 2,
        in_specs=[SMEM_WHOLE] + [HBM_WHOLE] * len(flat),
        out_specs=(VMEM_WHOLE,) * 2,
        scratch_shapes=[pltpu.VMEM((rows, width), BF16), pltpu.SemaphoreType.DMA((peers,))],
        compiler_params=vmem(),
        cost_estimate=small_cost,
        name="write_outputs",
    )(flags, *map(in_hbm, flat))


def solution(mesh):
    in_specs = (
        P(None, "tensor"),
        P(None, "tensor"),
        P("pipe", None),
        P("pipe", None, "tensor"),
        P("pipe", None, "tensor"),
        P("pipe", "tensor", None),
        P("pipe", None, None, "tensor"),
    )
    out_specs = (P("pipe", None, None), P("pipe", None, None))
    return jax.shard_map(local, mesh=mesh, in_specs=in_specs, out_specs=out_specs, check_vma=False)
```

```python
import functools

import jax
import jax.numpy as jnp
from jax import lax
from jax.experimental import pallas as pl
from jax.experimental.pallas import tpu as pltpu
from jax.sharding import PartitionSpec as P

BLOCK = 128
EPS = 1e-05
F32 = jnp.float32
BF16 = jnp.bfloat16
VMEM_WHOLE = pl.BlockSpec(memory_space=pltpu.VMEM)
SMEM_WHOLE = pl.BlockSpec(memory_space=pltpu.SMEM)
HBM_WHOLE = pl.BlockSpec(memory_space=pltpu.HBM)
FOUR_STAGE_SETS = (
    ((0, 2), (2, 1)),
    ((1, 2), (3, 1)),
    ((0, 1), (3, 2)),
    ((1, 3), (2, 0)),
)


def tile_of(size):
    return next(tile for tile in (256, 128) if size % tile == 0)


def contract_last(left, right):
    return lax.dot_general(left, right, (((1,), (1,)), ((), ())), preferred_element_type=F32)


def load_kernel(mask, gate_hbm, up_hbm, down_hbm, gate_out, up_out, down_out, wide_sems, deep_sems):
    width, cols = gate_out.shape
    parts = wide_sems.shape[1]
    size = width // parts
    wide_blocks, deep_blocks = width // BLOCK, cols // BLOCK
    pairs = ((gate_hbm, gate_out), (up_hbm, up_out))

    def wide(which, part):
        source, target = pairs[which]
        here = pl.ds(part * size, size)
        return pltpu.make_async_copy(source.at[0, here], target.at[here], wide_sems.at[which, part])

    def deep(col):
        here = pl.ds(col * BLOCK, BLOCK)
        return pltpu.make_async_copy(down_hbm.at[0, here], down_out.at[here], deep_sems.at[col])

    for which in range(2):
        for part in range(parts):
            wide(which, part).start()
    for col in range(deep_blocks):
        deep(col).start()
    zero = jnp.zeros((BLOCK, BLOCK), BF16)
    for which in range(2):
        ref = pairs[which][1]
        for part in range(parts):
            wide(which, part).wait()

            @pl.loop(part * (wide_blocks // parts), (part + 1) * (wide_blocks // parts))
            def _(row):
                for col in range(deep_blocks):

                    @pl.when(mask[(which * wide_blocks + row) * deep_blocks + col] == 0)
                    def _():
                        ref[pl.ds(row * BLOCK, BLOCK), col * BLOCK : (col + 1) * BLOCK] = zero

    for col in range(deep_blocks):
        deep(col).wait()

        @pl.loop(0, wide_blocks)
        def _(row):
            @pl.when(mask[(2 * wide_blocks + row) * deep_blocks + col] == 0)
            def _():
                down_out[col * BLOCK : (col + 1) * BLOCK, pl.ds(row * BLOCK, BLOCK)] = zero


def place_of(flags, peers, part, step):
    return pl.multiple_of(lax.rem(flags[1] + peers + step, peers) * part, part)


def row_scale(xval, peers):
    rows, width = xval.shape
    part = width // peers

    def square(index, total):
        here = xval[:, pl.ds(pl.multiple_of(index * part, part), part)].astype(F32)
        return total + jnp.sum(here * here, axis=1, keepdims=True)

    total = lax.fori_loop(0, peers, square, jnp.zeros((rows, 1), F32))
    return lax.rsqrt(total / width + EPS)


def pass_along(flags, source, extra, targets):
    if extra:

        @pl.when(flags[0] == source)
        def _():
            for step, target in enumerate(targets):
                target[...] = extra[step % len(extra)][...]


def forward_in_kernel(flags, gmat, umat, dmat, *refs, peers, stage, held, steps, ends):
    count = len(steps)
    pieces = refs[:count]
    gain = refs[count]
    xval, gate_store, up_store, *hidden, scaled = refs[count + 1 + held :]
    part = pieces[0].shape[1]
    width, cols = gmat.shape
    tile = tile_of(cols)

    @pl.when(flags[0] == stage)
    def _():
        places = [place_of(flags, peers, part, -step) for step in steps]
        for index, piece in enumerate(pieces):
            here = pl.ds(places[index], part)
            xval[:, here] = piece[...]
            scaled[index] = (piece[...].astype(F32) * gain[:, here]).astype(BF16)
        scale = row_scale(xval, peers) if ends else None

        @pl.loop(0, cols // tile)
        def _(number):
            here = pl.ds(pl.multiple_of(number * tile, tile), tile)
            totals = []
            for store, mat in ((gate_store, gmat), (up_store, umat)):
                total = store[:, here] if ends else None
                for index in range(count):
                    term = jnp.dot(
                        scaled[index], mat[pl.ds(places[index], part), here], preferred_element_type=F32
                    )
                    total = term if total is None else total + term
                if ends:
                    total = total * scale
                store[:, here] = total
                totals.append(total)
            if ends:
                gate, upper = totals
                hidden[0][:, here] = (gate * jax.nn.sigmoid(gate) * upper).astype(BF16)


def forward_out_kernel(flags, gmat, umat, dmat, *refs, peers, stage, steps, source, extras):
    hidden, xval = refs[:2]
    extra, partial = refs[2 : 2 + extras], refs[-len(steps) :]
    part = partial[0].shape[1]
    pass_along(flags, source, extra, partial)

    @pl.when(flags[0] == stage)
    def _():
        for step, target in zip(steps, partial):
            here = pl.ds(place_of(flags, peers, part, step), part)
            branch = jnp.dot(hidden[...], dmat[:, here], preferred_element_type=F32)
            if step == 0:
                branch = branch + xval[:, here].astype(F32)
            target[...] = branch.astype(BF16)


def backward_in_kernel(flags, gmat, umat, dmat, *refs, peers, stage, held, steps, ends):
    count = len(steps)
    pieces = refs[:count]
    xval, gate_store, up_store = refs[count : count + 3]
    cot, dhid_store, *outs = refs[count + 3 + held :]
    part = pieces[0].shape[1]
    rows, width = xval.shape
    cols = dmat.shape[0]
    tile = tile_of(cols)

    @pl.when(flags[0] == stage)
    def _():
        places = [place_of(flags, peers, part, -step) for step in steps]
        for index, piece in enumerate(pieces):
            cot[:, pl.ds(places[index], part)] = piece[...]

        def hidden_side(number, inner):
            here = pl.ds(pl.multiple_of(number * tile, tile), tile)
            dhid = dhid_store[:, here] if ends else None
            for index, piece in enumerate(pieces):
                term = contract_last(piece[...], dmat[here, pl.ds(places[index], part)])
                dhid = term if dhid is None else dhid + term
            if not ends:
                dhid_store[:, here] = dhid
                return inner
            gate = gate_store[:, here]
            upper = up_store[:, here]
            sig = jax.nn.sigmoid(gate)
            dgate_low = (dhid * upper * sig * (1.0 + gate * (1.0 - sig))).astype(BF16)
            dup_low = (dhid * gate * sig).astype(BF16)
            outs[0][:, here] = dgate_low
            outs[1][:, here] = dup_low
            both = dgate_low.astype(F32) * gate + dup_low.astype(F32) * upper
            return inner + jnp.sum(both, axis=1, keepdims=True)

        inner = lax.fori_loop(0, cols // tile, hidden_side, jnp.zeros((rows, 1), F32))
        if ends:
            scale = row_scale(xval, peers)
            lanes = outs[2].shape[1] // 2
            outs[2][:, :lanes] = jnp.broadcast_to(scale, (rows, lanes))
            outs[2][:, lanes:] = jnp.broadcast_to(scale * scale * inner / width, (rows, lanes))


def backward_out_kernel(flags, gmat, umat, dmat, *refs, peers, stage, steps, source, extras):
    dgate, dup, scales, xval, cot, gain = refs[:6]
    extra, partial = refs[6 : 6 + extras], refs[-len(steps) :]
    part = partial[0].shape[1]
    pass_along(flags, source, extra, partial)

    @pl.when(flags[0] == stage)
    def _():
        lanes = scales.shape[1] // 2
        scale, pull = scales[:, :1], scales[:, lanes : lanes + 1]
        for step, target in zip(steps, partial):
            here = pl.ds(place_of(flags, peers, part, step), part)
            dnorm = contract_last(dgate[...], gmat[here, :]) + contract_last(dup[...], umat[here, :])
            back = scale * (dnorm * gain[:, here]) - xval[:, here].astype(F32) * pull
            if step == 0:
                back = back + cot[:, here].astype(F32)
            target[...] = back.astype(BF16)


def sum_kernel(flags, *refs, peers, owners, source):
    pieces, extra, out = refs[:peers], refs[peers:-1], refs[-1]
    active = functools.reduce(jnp.logical_or, [flags[0] == owner for owner in owners])

    @pl.when(active)
    def _():
        total = pieces[0][...].astype(F32)
        for piece in pieces[1:]:
            total = total + piece[...].astype(F32)
        out[...] = total.astype(BF16)

    pass_along(flags, source, extra, [out])


def outputs_kernel(flags, *refs, peers, counts):
    *sources, section_out, section_grad, low, high, in_sems, out_sems = refs
    rows, width = low.shape[1:]
    part = width // peers
    start = 0
    for stage in range(len(counts) // 2):
        held = []
        for count in counts[2 * stage : 2 * stage + 2]:
            held.append(sources[start : start + count])
            start += count

        @pl.when(flags[0] == stage)
        def _():
            brought, written = [], []
            for which, given in enumerate(held):
                for step, source in enumerate(given):
                    target = low.at[which]
                    if len(given) > 1:
                        target = target.at[:, pl.ds(place_of(flags, peers, part, -step), part)]
                    brought.append(pltpu.make_async_copy(source, target, in_sems.at[which, step]))
                    brought[-1].start()
            for which, given in enumerate(held):
                for step in range(peers):
                    if step < len(given):
                        brought.pop(0).wait()
                    here = pl.ds(place_of(flags, peers, part, -step), part)
                    high[which, :, here] = low[which, :, here].astype(F32)
                    written.append(
                        pltpu.make_async_copy(
                            high.at[which, :, here],
                            (section_out, section_grad)[which].at[0, :, here],
                            out_sems.at[which, step],
                        )
                    )
                    written[-1].start()
            for copy in written:
                copy.wait()


def local(inputs, out_grad, norm_gain, gate_weight, up_weight, down_weight, block_mask):
    stages, peers = lax.axis_size("pipe"), lax.axis_size("tensor")
    stage, peer = lax.axis_index("pipe"), lax.axis_index("tensor")
    rows, part = inputs.shape
    width, cols = gate_weight.shape[1:]
    final = stages - 1
    flags = jnp.stack([stage, peer]).astype(jnp.int32)
    vmem = functools.partial(pltpu.CompilerParams, vmem_limit_bytes=12 * 2**20)
    in_vmem = functools.partial(pltpu.with_memory_space_constraint, memory_space=pltpu.VMEM)
    in_hbm = functools.partial(pltpu.with_memory_space_constraint, memory_space=pltpu.HBM)

    if stages == 4:
        sets = FOUR_STAGE_SETS
    else:
        sets = tuple(((a, b),) for a in range(stages) for b in range(stages) if a != b)
    hops = [hop for group in sets for hop in group]

    def set_of(hop):
        return next(group for group in sets if hop in group)

    def owner_of(source, target):
        return next(o for o in range(stages) if (source, o) in hops and (o, target) in hops)

    def moved(value, hop, step):
        pairs = [
            (source * peers + who, target * peers + (who + step) % peers)
            for source, target in set_of(hop)
            for who in range(peers)
        ]
        return lax.ppermute(value, ("pipe", "tensor"), pairs)

    def spread(values, hop):
        return [moved(values[step % len(values)], hop, step) for step in range(peers)]

    waiting = []

    def fellow(hop):
        for entry in waiting:
            if entry[0] != hop and entry[0] in set_of(hop):
                waiting[:] = [other for other in waiting if other is not entry]
                return entry[:3]
        return (None, None), [], lambda arrived: None

    def piece_type():
        return pltpu.VMEM((rows, part), BF16)

    weights = pl.pallas_call(
        load_kernel,
        out_shape=(
            pltpu.VMEM((width, cols), BF16),
            pltpu.VMEM((width, cols), BF16),
            pltpu.VMEM((cols, width), BF16),
        ),
        in_specs=[SMEM_WHOLE] + [HBM_WHOLE] * 3,
        out_specs=(VMEM_WHOLE,) * 3,
        scratch_shapes=[
            pltpu.SemaphoreType.DMA((2, 8)),
            pltpu.SemaphoreType.DMA((cols // BLOCK,)),
        ],
        compiler_params=vmem(vmem_limit_bytes=13 * 2**20),
        cost_estimate=pl.CostEstimate(flops=0, bytes_accessed=6 * width * cols, transcendentals=0),
        name="load_masked",
    )(block_mask.reshape(-1), gate_weight, up_weight, down_weight)
    weights = [in_vmem(weight) for weight in weights]

    small_cost = pl.CostEstimate(flops=0, bytes_accessed=4 * rows * width, transcendentals=0)
    hidden_type = pltpu.VMEM((rows, cols), F32)
    wide_type = pltpu.VMEM((rows, width), BF16)

    order = sorted(range(peers), key=lambda step: (abs(2 * step - peers), step))
    halves = (tuple(order[: peers // 2]), tuple(order[peers // 2 :]))

    def called(kernel, operands, carried, out_types, scratch, name, share, **known):
        held_from = 1 + len(weights) + len(operands)
        return pl.pallas_call(
            functools.partial(kernel, peers=peers, **known),
            out_shape=tuple(out_types),
            in_specs=[SMEM_WHOLE] * 1 + [VMEM_WHOLE] * (len(weights) + len(operands) + len(carried)),
            out_specs=(VMEM_WHOLE,) * len(out_types),
            scratch_shapes=scratch,
            input_output_aliases={held_from + index: index for index in range(len(carried))},
            compiler_params=vmem(vmem_limit_bytes=13 * 2**20),
            cost_estimate=pl.CostEstimate(
                flops=int(share * 2 * rows * width * cols),
                bytes_accessed=int(share * 2 * width * cols),
                transcendentals=0,
            ),
            name=name,
        )(flags, *weights, *map(in_vmem, operands), *map(in_vmem, carried))

    def pieces_out(kernel, at, operands, source, extra, groups, share, name):
        partial = [None] * peers
        for steps in groups:
            own = [extra[step % len(extra)] for step in steps] if len(extra) > 1 else list(extra)
            outs = called(
                kernel, [*operands, *own], [], [piece_type() for _ in steps], [], name,
                share * len(steps) / peers, stage=at, steps=steps, source=source, extras=len(own),
            )
            for step, out in zip(steps, outs):
                partial[step] = out
        return partial

    def summed(pieces, owners, source=None, extra=()):
        return pl.pallas_call(
            functools.partial(sum_kernel, peers=peers, owners=owners, source=source),
            out_shape=piece_type(),
            in_specs=[SMEM_WHOLE] + [VMEM_WHOLE] * (peers + len(extra)),
            out_specs=VMEM_WHOLE,
            compiler_params=vmem(vmem_limit_bytes=2*2**20),
            cost_estimate=small_cost,
            name="sum_pieces",
        )(flags, *map(in_vmem, pieces), *map(in_vmem, extra))

    section_out, section_grad = [None] * stages, [None] * stages

    def keep_in(store, at):
        def arrive(arrived):
            store[at] = arrived

        return arrive

    def handed(at, target, run, store):
        owner = owner_of(at, target)
        (source, _), extra, arrive = fellow((at, owner))
        pieces = spread(run(source, extra), (at, owner))
        late = arrive(pieces)
        (source, _), extra, arrive = fellow((owner, target))
        if late is not None and (late, final) in set_of((owner, target)) and not extra:
            shard = summed(pieces, (owner, late))
            arrive = keep_in(section_out, final)
        else:
            shard = summed(pieces, (owner,), source, extra)
            if late is not None:
                waiting.append(
                    ((late, final), [summed(pieces, (late,))], keep_in(section_out, final), None)
                )
        if target != at:
            waiting.append(((owner, at), [shard], keep_in(store, at), store))
        got = spread([shard], (owner, target))
        arrive(got)
        return got

    first_from = next(a for a, b in hops if b == 0)
    last_from = next(a for a, b in hops if b == final)
    if set_of((first_from, 0)) == set_of((last_from, final)):
        first = jnp.where(stage == last_from, out_grad, inputs)
        pieces = last_pieces = spread([first], (first_from, 0))
    else:
        pieces, last_pieces = spread([inputs], (first_from, 0)), spread([out_grad], (last_from, final))

    kept = []
    gmat, umat, dmat = weights

    def forward_in(at, pieces):
        nonlocal kept
        for steps in halves:
            ends = steps is halves[-1]
            types = [wide_type, hidden_type, hidden_type] + [pltpu.VMEM((rows, cols), BF16)] * ends
            outs = called(
                forward_in_kernel, [*(pieces[step] for step in steps), norm_gain], kept, types,
                [pltpu.VMEM((len(steps), rows, part), BF16)], "forward_in", 1.0,
                stage=at, held=len(kept), steps=steps, ends=ends,
            )
            kept = outs[:3]
        return outs[3]

    def forward_out(at, hidden, xval, source, extra):
        return pieces_out(
            forward_out_kernel, at, [hidden, xval], source, extra, halves, 1.0, "forward_out"
        )

    def run_forward(at, pieces, source, extra):
        return forward_out(at, forward_in(at, pieces), kept[0], source, extra)

    for at in range(final):
        pieces = handed(at, at + 1, functools.partial(run_forward, at, pieces), section_out)
    last_hidden = forward_in(final, pieces)

    cot = []
    quarters = tuple(half[at : at + max(1, peers // 4)] for half in halves for at in range(0, len(half), max(1, peers // 4)))

    def run_backward(at, pieces, source, extra):
        nonlocal cot
        low_type = pltpu.VMEM((rows, cols), BF16)
        for steps in halves:
            ends = steps is halves[-1]
            types = [wide_type, hidden_type] + [low_type, low_type, pltpu.VMEM((rows, 2 * BLOCK), F32)] * ends
            outs = called(
                backward_in_kernel, [*(pieces[step] for step in steps), *kept], cot, types, [],
                "backward_in", 0.5, stage=at, held=len(cot), steps=steps, ends=ends,
            )
            cot = outs[:2]
        partial = pieces_out(
            backward_out_kernel, at, [*outs[2:], kept[0], cot[0], norm_gain],
            source, extra, quarters, 2.0, "backward_out",
        )
        if at == final:
            last_owner = owner_of(final, final)
            hidden, xval, *_ = lax.optimization_barrier((last_hidden, kept[0], partial[order[-1]]))
            last_partial = forward_out(final, hidden, xval, None, [])
            waiting.append(((final, last_owner), last_partial, lambda arrived: last_owner, None))
        return partial

    pieces = last_pieces
    for at in range(final, -1, -1):
        pieces = handed(at, max(at - 1, 0), functools.partial(run_backward, at, pieces), section_grad)
        for entry in tuple(waiting):
            if at and entry[0][1] == at + 1 and entry[3] is section_grad and (at, at + 1) in hops:
                waiting[:] = [other for other in waiting if other is not entry]
                section_grad[at + 1] = [moved(cot[0], (at, at + 1), 0)]
    section_grad[0] = pieces

    while waiting:
        hop, values, arrive, _ = waiting.pop(0)
        arrived = spread(values, hop)
        late = arrive(arrived)
        if late is not None:
            waiting.append(((late, final), [summed(arrived, (late,))], keep_in(section_out, final), None))

    sources = [store[at] for at in range(stages) for store in (section_out, section_grad)]
    flat = [value for source in sources for value in source]
    return pl.pallas_call(
        functools.partial(outputs_kernel, peers=peers, counts=[len(source) for source in sources]),
        out_shape=(jax.ShapeDtypeStruct((1, rows, width), F32),) * 2,
        in_specs=[SMEM_WHOLE] + [HBM_WHOLE] * len(flat),
        out_specs=(HBM_WHOLE,) * 2,
        scratch_shapes=[
            pltpu.VMEM((2, rows, width), BF16),
            pltpu.VMEM((2, rows, width), F32),
            pltpu.SemaphoreType.DMA((2, peers)),
            pltpu.SemaphoreType.DMA((2, peers)),
        ],
        compiler_params=vmem(),
        cost_estimate=small_cost,
        name="write_outputs",
    )(flags, *map(in_hbm, flat))


def solution(mesh):
    in_specs = (
        P(None, "tensor"),
        P(None, "tensor"),
        P("pipe", None),
        P("pipe", None, "tensor"),
        P("pipe", None, "tensor"),
        P("pipe", "tensor", None),
        P("pipe", None, None, "tensor"),
    )
    out_specs = (P("pipe", None, None), P("pipe", None, None))
    return jax.shard_map(local, mesh=mesh, in_specs=in_specs, out_specs=out_specs, check_vma=False)
```

```python
import functools

import jax
import jax.numpy as jnp
from jax import lax
from jax.experimental import pallas as pl
from jax.experimental.pallas import tpu as pltpu
from jax.sharding import PartitionSpec as P

BLOCK = 128
EPS = 1e-05
F32 = jnp.float32
BF16 = jnp.bfloat16
VMEM_WHOLE = pl.BlockSpec(memory_space=pltpu.VMEM)
SMEM_WHOLE = pl.BlockSpec(memory_space=pltpu.SMEM)
HBM_WHOLE = pl.BlockSpec(memory_space=pltpu.HBM)
FOUR_STAGE_SETS = (
    ((0, 2), (2, 1)),
    ((1, 2), (3, 1)),
    ((0, 1), (3, 2)),
    ((1, 3), (2, 0)),
)


def tile_of(size):
    return next(tile for tile in (256, 128) if size % tile == 0)


def contract_last(left, right):
    return lax.dot_general(left, right, (((1,), (1,)), ((), ())), preferred_element_type=F32)


def load_kernel(mask, gate_hbm, up_hbm, down_hbm, gate_out, up_out, down_out, wide_sems, deep_sems):
    width, cols = gate_out.shape
    parts = wide_sems.shape[1]
    size = width // parts
    wide_blocks, deep_blocks = width // BLOCK, cols // BLOCK
    pairs = ((gate_hbm, gate_out), (up_hbm, up_out))

    def wide(which, part):
        source, target = pairs[which]
        here = pl.ds(part * size, size)
        return pltpu.make_async_copy(source.at[0, here], target.at[here], wide_sems.at[which, part])

    def deep(col):
        here = pl.ds(col * BLOCK, BLOCK)
        return pltpu.make_async_copy(down_hbm.at[0, here], down_out.at[here], deep_sems.at[col])

    for which in range(2):
        for part in range(parts):
            wide(which, part).start()
    for col in range(deep_blocks):
        deep(col).start()

    def keep(ref, row, col, number):
        factor = jnp.full((16, BLOCK), mask[number].astype(F32), F32).astype(BF16)
        for below in range(0, BLOCK, 16):
            here = (pl.ds(row + below, 16), pl.ds(col, BLOCK))
            ref[here] = ref[here] * factor

    for which in range(2):
        ref = pairs[which][1]
        for part in range(parts):
            wide(which, part).wait()

            @pl.loop(part * (wide_blocks // parts), (part + 1) * (wide_blocks // parts))
            def _(row):
                for col in range(deep_blocks):
                    keep(ref, pl.multiple_of(row * BLOCK, BLOCK), col * BLOCK, (which * wide_blocks + row) * deep_blocks + col)

    for col in range(deep_blocks):
        deep(col).wait()

        @pl.loop(0, wide_blocks // 8)
        def _(group):
            for row in range(8):
                number = (2 * wide_blocks + group * 8 + row) * deep_blocks + col
                place = pl.multiple_of((group * 8 + row) * BLOCK, BLOCK)
                keep(down_out, col * BLOCK, place, number)


def place_of(flags, peers, part, step):
    return pl.multiple_of(lax.rem(flags[1] + peers + step, peers) * part, part)


def row_scale(xval, peers):
    rows, width = xval.shape
    part = width // peers

    def square(index, total):
        here = xval[:, pl.ds(pl.multiple_of(index * part, part), part)].astype(F32)
        return total + jnp.sum(here * here, axis=1, keepdims=True)

    total = lax.fori_loop(0, peers, square, jnp.zeros((rows, 1), F32))
    return lax.rsqrt(total / width + EPS)


def pass_along(flags, source, extra, targets):
    if extra:

        @pl.when(flags[0] == source)
        def _():
            for step, target in enumerate(targets):
                target[...] = extra[step % len(extra)][...]


def forward_in_kernel(flags, gmat, umat, dmat, *refs, peers, stage, held, steps, ends):
    count = len(steps)
    pieces = refs[:count]
    gain = refs[count]
    xval, gate_store, up_store, *hidden, scaled = refs[count + 1 + held :]
    part = pieces[0].shape[1]
    width, cols = gmat.shape
    tile = tile_of(cols)

    @pl.when(flags[0] == stage)
    def _():
        places = [place_of(flags, peers, part, -step) for step in steps]
        for index, piece in enumerate(pieces):
            here = pl.ds(places[index], part)
            xval[:, here] = piece[...]
            scaled[index] = (piece[...].astype(F32) * gain[:, here]).astype(BF16)
        scale = row_scale(xval, peers) if ends else None

        @pl.loop(0, cols // tile)
        def _(number):
            here = pl.ds(pl.multiple_of(number * tile, tile), tile)
            totals = []
            for store, mat in ((gate_store, gmat), (up_store, umat)):
                total = store[:, here] if ends else None
                for index in range(count):
                    term = jnp.dot(
                        scaled[index], mat[pl.ds(places[index], part), here], preferred_element_type=F32
                    )
                    total = term if total is None else total + term
                if ends:
                    total = total * scale
                store[:, here] = total
                totals.append(total)
            if ends:
                gate, upper = totals
                hidden[0][:, here] = (gate * jax.nn.sigmoid(gate) * upper).astype(BF16)


def forward_out_kernel(flags, gmat, umat, dmat, *refs, peers, stage, steps, source, extras):
    hidden, xval = refs[:2]
    extra, partial = refs[2 : 2 + extras], refs[-len(steps) :]
    part = partial[0].shape[1]
    pass_along(flags, source, extra, partial)

    @pl.when(flags[0] == stage)
    def _():
        for step, target in zip(steps, partial):
            here = pl.ds(place_of(flags, peers, part, step), part)
            branch = jnp.dot(hidden[...], dmat[:, here], preferred_element_type=F32)
            if step == 0:
                branch = branch + xval[:, here].astype(F32)
            target[...] = branch.astype(BF16)


def backward_in_kernel(flags, gmat, umat, dmat, *refs, peers, stage, held, steps, ends):
    count = len(steps)
    pieces = refs[:count]
    xval, gate_store, up_store = refs[count : count + 3]
    cot, dhid_store, *outs = refs[count + 3 + held :]
    part = pieces[0].shape[1]
    rows, width = xval.shape
    cols = dmat.shape[0]
    tile = tile_of(cols)

    @pl.when(flags[0] == stage)
    def _():
        places = [place_of(flags, peers, part, -step) for step in steps]
        for index, piece in enumerate(pieces):
            cot[:, pl.ds(places[index], part)] = piece[...]

        def hidden_side(number, inner):
            here = pl.ds(pl.multiple_of(number * tile, tile), tile)
            dhid = dhid_store[:, here] if ends else None
            for index, piece in enumerate(pieces):
                term = contract_last(piece[...], dmat[here, pl.ds(places[index], part)])
                dhid = term if dhid is None else dhid + term
            if not ends:
                dhid_store[:, here] = dhid
                return inner
            gate = gate_store[:, here]
            upper = up_store[:, here]
            sig = jax.nn.sigmoid(gate)
            dgate_low = (dhid * upper * sig * (1.0 + gate * (1.0 - sig))).astype(BF16)
            dup_low = (dhid * gate * sig).astype(BF16)
            outs[0][:, here] = dgate_low
            outs[1][:, here] = dup_low
            both = dgate_low.astype(F32) * gate + dup_low.astype(F32) * upper
            return inner + jnp.sum(both, axis=1, keepdims=True)

        inner = lax.fori_loop(0, cols // tile, hidden_side, jnp.zeros((rows, 1), F32))
        if ends:
            scale = row_scale(xval, peers)
            lanes = outs[2].shape[1] // 2
            outs[2][:, :lanes] = jnp.broadcast_to(scale, (rows, lanes))
            outs[2][:, lanes:] = jnp.broadcast_to(scale * scale * inner / width, (rows, lanes))


def backward_out_kernel(flags, gmat, umat, dmat, *refs, peers, stage, steps, source, extras):
    dgate, dup, scales, xval, cot, gain = refs[:6]
    extra, partial = refs[6 : 6 + extras], refs[-len(steps) :]
    part = partial[0].shape[1]
    pass_along(flags, source, extra, partial)

    @pl.when(flags[0] == stage)
    def _():
        lanes = scales.shape[1] // 2
        scale, pull = scales[:, :1], scales[:, lanes : lanes + 1]
        for step, target in zip(steps, partial):
            here = pl.ds(place_of(flags, peers, part, step), part)
            dnorm = contract_last(dgate[...], gmat[here, :]) + contract_last(dup[...], umat[here, :])
            back = scale * (dnorm * gain[:, here]) - xval[:, here].astype(F32) * pull
            if step == 0:
                back = back + cot[:, here].astype(F32)
            target[...] = back.astype(BF16)


def sum_kernel(flags, *refs, peers, owners, source):
    pieces, extra, out = refs[:peers], refs[peers:-1], refs[-1]
    active = functools.reduce(jnp.logical_or, [flags[0] == owner for owner in owners])

    @pl.when(active)
    def _():
        total = pieces[0][...].astype(F32)
        for piece in pieces[1:]:
            total = total + piece[...].astype(F32)
        out[...] = total.astype(BF16)

    pass_along(flags, source, extra, [out])


def outputs_kernel(flags, *refs, peers, counts):
    *sources, section_out, section_grad, low, high, in_sems, out_sems = refs
    rows, width = low.shape[1:]
    part = width // peers
    start = 0
    for stage in range(len(counts) // 2):
        held = []
        for count in counts[2 * stage : 2 * stage + 2]:
            held.append(sources[start : start + count])
            start += count

        @pl.when(flags[0] == stage)
        def _():
            brought, written = [], []
            for which, given in enumerate(held):
                for step, source in enumerate(given):
                    target = low.at[which]
                    if len(given) > 1:
                        target = target.at[:, pl.ds(place_of(flags, peers, part, -step), part)]
                    brought.append(pltpu.make_async_copy(source, target, in_sems.at[which, step]))
                    brought[-1].start()
            for which, given in enumerate(held):
                for step in range(peers):
                    if step < len(given):
                        brought.pop(0).wait()
                    here = pl.ds(place_of(flags, peers, part, -step), part)
                    high[which, :, here] = low[which, :, here].astype(F32)
                    written.append(
                        pltpu.make_async_copy(
                            high.at[which, :, here],
                            (section_out, section_grad)[which].at[0, :, here],
                            out_sems.at[which, step],
                        )
                    )
                    written[-1].start()
            for copy in written:
                copy.wait()


def local(inputs, out_grad, norm_gain, gate_weight, up_weight, down_weight, block_mask):
    stages, peers = lax.axis_size("pipe"), lax.axis_size("tensor")
    stage, peer = lax.axis_index("pipe"), lax.axis_index("tensor")
    rows, part = inputs.shape
    width, cols = gate_weight.shape[1:]
    final = stages - 1
    flags = jnp.stack([stage, peer]).astype(jnp.int32)
    vmem = functools.partial(pltpu.CompilerParams, vmem_limit_bytes=12 * 2**20)
    in_vmem = functools.partial(pltpu.with_memory_space_constraint, memory_space=pltpu.VMEM)
    in_hbm = functools.partial(pltpu.with_memory_space_constraint, memory_space=pltpu.HBM)

    if stages == 4:
        sets = FOUR_STAGE_SETS
    else:
        sets = tuple(((a, b),) for a in range(stages) for b in range(stages) if a != b)
    hops = [hop for group in sets for hop in group]

    def set_of(hop):
        return next(group for group in sets if hop in group)

    def owner_of(source, target):
        return next(o for o in range(stages) if (source, o) in hops and (o, target) in hops)

    def moved(value, hop, step):
        pairs = [
            (source * peers + who, target * peers + (who + step) % peers)
            for source, target in set_of(hop)
            for who in range(peers)
        ]
        return lax.ppermute(value, ("pipe", "tensor"), pairs)

    def spread(values, hop):
        return [moved(values[step % len(values)], hop, step) for step in range(peers)]

    waiting = []

    def fellow(hop):
        for entry in waiting:
            if entry[0] != hop and entry[0] in set_of(hop):
                waiting[:] = [other for other in waiting if other is not entry]
                return entry[:3]
        return (None, None), [], lambda arrived: None

    def piece_type():
        return pltpu.VMEM((rows, part), BF16)

    weights = pl.pallas_call(
        load_kernel,
        out_shape=(
            pltpu.VMEM((width, cols), BF16),
            pltpu.VMEM((width, cols), BF16),
            pltpu.VMEM((cols, width), BF16),
        ),
        in_specs=[SMEM_WHOLE] + [HBM_WHOLE] * 3,
        out_specs=(VMEM_WHOLE,) * 3,
        scratch_shapes=[
            pltpu.SemaphoreType.DMA((2, 8)),
            pltpu.SemaphoreType.DMA((cols // BLOCK,)),
        ],
        compiler_params=vmem(vmem_limit_bytes=13 * 2**20),
        cost_estimate=pl.CostEstimate(flops=0, bytes_accessed=6 * width * cols, transcendentals=0),
        name="load_masked",
    )(block_mask.reshape(-1), gate_weight, up_weight, down_weight)
    weights = [in_vmem(weight) for weight in weights]

    small_cost = pl.CostEstimate(flops=0, bytes_accessed=4 * rows * width, transcendentals=0)
    hidden_type = pltpu.VMEM((rows, cols), F32)
    wide_type = pltpu.VMEM((rows, width), BF16)

    order = sorted(range(peers), key=lambda step: (abs(2 * step - peers), step))
    halves = (tuple(order[: peers // 2]), tuple(order[peers // 2 :]))

    def called(kernel, operands, carried, out_types, scratch, name, share, **known):
        held_from = 1 + len(weights) + len(operands)
        return pl.pallas_call(
            functools.partial(kernel, peers=peers, **known),
            out_shape=tuple(out_types),
            in_specs=[SMEM_WHOLE] * 1 + [VMEM_WHOLE] * (len(weights) + len(operands) + len(carried)),
            out_specs=(VMEM_WHOLE,) * len(out_types),
            scratch_shapes=scratch,
            input_output_aliases={held_from + index: index for index in range(len(carried))},
            compiler_params=vmem(vmem_limit_bytes=13 * 2**20),
            cost_estimate=pl.CostEstimate(
                flops=int(share * 2 * rows * width * cols),
                bytes_accessed=int(share * 2 * width * cols),
                transcendentals=0,
            ),
            name=name,
        )(flags, *weights, *map(in_vmem, operands), *map(in_vmem, carried))

    def pieces_out(kernel, at, operands, source, extra, groups, share, name):
        partial = [None] * peers
        for steps in groups:
            own = [extra[step % len(extra)] for step in steps] if len(extra) > 1 else list(extra)
            outs = called(
                kernel, [*operands, *own], [], [piece_type() for _ in steps], [], name,
                share * len(steps) / peers, stage=at, steps=steps, source=source, extras=len(own),
            )
            for step, out in zip(steps, outs):
                partial[step] = out
        return partial

    def summed(pieces, owners, source=None, extra=()):
        return pl.pallas_call(
            functools.partial(sum_kernel, peers=peers, owners=owners, source=source),
            out_shape=piece_type(),
            in_specs=[SMEM_WHOLE] + [VMEM_WHOLE] * (peers + len(extra)),
            out_specs=VMEM_WHOLE,
            compiler_params=vmem(vmem_limit_bytes=2*2**20),
            cost_estimate=small_cost,
            name="sum_pieces",
        )(flags, *map(in_vmem, pieces), *map(in_vmem, extra))

    section_out, section_grad = [None] * stages, [None] * stages

    def keep_in(store, at):
        def arrive(arrived):
            store[at] = arrived

        return arrive

    def handed(at, target, run, store):
        owner = owner_of(at, target)
        (source, _), extra, arrive = fellow((at, owner))
        pieces = spread(run(source, extra), (at, owner))
        late = arrive(pieces)
        (source, _), extra, arrive = fellow((owner, target))
        if late is not None and (late, final) in set_of((owner, target)) and not extra:
            shard = summed(pieces, (owner, late))
            arrive = keep_in(section_out, final)
        else:
            shard = summed(pieces, (owner,), source, extra)
            if late is not None:
                waiting.append(
                    ((late, final), [summed(pieces, (late,))], keep_in(section_out, final), None)
                )
        if target != at:
            waiting.append(((owner, at), [shard], keep_in(store, at), store))
        got = spread([shard], (owner, target))
        arrive(got)
        return got

    first_from = next(a for a, b in hops if b == 0)
    last_from = next(a for a, b in hops if b == final)
    if set_of((first_from, 0)) == set_of((last_from, final)):
        first = jnp.where(stage == last_from, out_grad, inputs)
        pieces = last_pieces = spread([first], (first_from, 0))
    else:
        pieces, last_pieces = spread([inputs], (first_from, 0)), spread([out_grad], (last_from, final))

    kept = []
    gmat, umat, dmat = weights

    def forward_in(at, pieces):
        nonlocal kept
        for steps in halves:
            ends = steps is halves[-1]
            types = [wide_type, hidden_type, hidden_type] + [pltpu.VMEM((rows, cols), BF16)] * ends
            outs = called(
                forward_in_kernel, [*(pieces[step] for step in steps), norm_gain], kept, types,
                [pltpu.VMEM((len(steps), rows, part), BF16)], "forward_in", 1.0,
                stage=at, held=len(kept), steps=steps, ends=ends,
            )
            kept = outs[:3]
        return outs[3]

    def forward_out(at, hidden, xval, source, extra):
        return pieces_out(
            forward_out_kernel, at, [hidden, xval], source, extra, halves, 1.0, "forward_out"
        )

    def run_forward(at, pieces, source, extra):
        return forward_out(at, forward_in(at, pieces), kept[0], source, extra)

    for at in range(final):
        pieces = handed(at, at + 1, functools.partial(run_forward, at, pieces), section_out)
    last_hidden = forward_in(final, pieces)

    cot = []
    quarters = tuple(half[at : at + max(1, peers // 4)] for half in halves for at in range(0, len(half), max(1, peers // 4)))

    def run_backward(at, pieces, source, extra):
        nonlocal cot
        low_type = pltpu.VMEM((rows, cols), BF16)
        for steps in halves:
            ends = steps is halves[-1]
            types = [wide_type, hidden_type] + [low_type, low_type, pltpu.VMEM((rows, 2 * BLOCK), F32)] * ends
            outs = called(
                backward_in_kernel, [*(pieces[step] for step in steps), *kept], cot, types, [],
                "backward_in", 0.5, stage=at, held=len(cot), steps=steps, ends=ends,
            )
            cot = outs[:2]
        partial = pieces_out(
            backward_out_kernel, at, [*outs[2:], kept[0], cot[0], norm_gain],
            source, extra, quarters, 2.0, "backward_out",
        )
        if at == final:
            last_owner = owner_of(final, final)
            hidden, xval, *_ = lax.optimization_barrier((last_hidden, kept[0], partial[order[-1]]))
            last_partial = forward_out(final, hidden, xval, None, [])
            waiting.append(((final, last_owner), last_partial, lambda arrived: last_owner, None))
        return partial

    pieces = last_pieces
    for at in range(final, -1, -1):
        pieces = handed(at, max(at - 1, 0), functools.partial(run_backward, at, pieces), section_grad)
        for entry in tuple(waiting):
            if at and entry[0][1] == at + 1 and entry[3] is section_grad and (at, at + 1) in hops:
                waiting[:] = [other for other in waiting if other is not entry]
                section_grad[at + 1] = [moved(cot[0], (at, at + 1), 0)]
    section_grad[0] = pieces

    while waiting:
        hop, values, arrive, _ = waiting.pop(0)
        arrived = spread(values, hop)
        late = arrive(arrived)
        if late is not None:
            waiting.append(((late, final), [summed(arrived, (late,))], keep_in(section_out, final), None))

    sources = [store[at] for at in range(stages) for store in (section_out, section_grad)]
    flat = [value for source in sources for value in source]
    return pl.pallas_call(
        functools.partial(outputs_kernel, peers=peers, counts=[len(source) for source in sources]),
        out_shape=(jax.ShapeDtypeStruct((1, rows, width), F32),) * 2,
        in_specs=[SMEM_WHOLE] + [HBM_WHOLE] * len(flat),
        out_specs=(HBM_WHOLE,) * 2,
        scratch_shapes=[
            pltpu.VMEM((2, rows, width), BF16),
            pltpu.VMEM((2, rows, width), F32),
            pltpu.SemaphoreType.DMA((2, peers)),
            pltpu.SemaphoreType.DMA((2, peers)),
        ],
        compiler_params=vmem(),
        cost_estimate=small_cost,
        name="write_outputs",
    )(flags, *map(in_hbm, flat))


def solution(mesh):
    in_specs = (
        P(None, "tensor"),
        P(None, "tensor"),
        P("pipe", None),
        P("pipe", None, "tensor"),
        P("pipe", None, "tensor"),
        P("pipe", "tensor", None),
        P("pipe", None, None, "tensor"),
    )
    out_specs = (P("pipe", None, None), P("pipe", None, None))
    return jax.shard_map(local, mesh=mesh, in_specs=in_specs, out_specs=out_specs, check_vma=False)
```
